128 devices in a mesh: tile: 32 (over z, y, core), dom: 4 (over x).
Axes of the slice: x: 4, y: 4, z: 4, core: 2. Of those that a mesh axis runs over, the one named last changes fastest.
Arguments:
- grid_latent: bfloat16 [262144, 512], P(('tile', 'dom')), may hold values from -6 to 6
- mesh_latent: bfloat16 [131072, 512], P(('tile', 'dom')), may hold values from -6 to 6
- g2m_send: int32 [128, 128], P(('tile', 'dom')), may hold values from 0 to 31
- g2m_src: int32 [128, 224], P(('tile', 'dom')), may hold values from 0 to 159, as said below
- g2m_dst: int32 [128, 224], P(('tile', 'dom')), may hold values from 0 to 15, as said below
- g2m_weight: bfloat16 [28672, 64, 64], P(('tile', 'dom')), may hold values from -0.1875 to 0.1875
- halo_send: int32 [128, 8], P(('tile', 'dom')), may hold values from 0 to 15
- m2m_src: int32 [128, 112], P(('tile', 'dom')), may hold values from 0 to 31, as said below
- m2m_dst: int32 [128, 112], P(('tile', 'dom')), may hold values from 0 to 15, as said below
- m2m_weight: bfloat16 [2, 14336, 64, 64], P(None, ('tile', 'dom')), may hold values from -0.25 to 0.25
- enc_msg_in: bfloat16 [512, 512], replicated, may hold values from -0.25 to 0.25
- enc_msg_out: bfloat16 [512, 512], replicated, may hold values from -0.25 to 0.25
- enc_upd_in: bfloat16 [1024, 512], replicated, may hold values from -0.1875 to 0.1875
- enc_upd_out: bfloat16 [512, 512], replicated, may hold values from -0.25 to 0.25
- enc_gain: float32 [512], replicated, may hold values from 0.1 to 1.9
- proc_msg_in: bfloat16 [2, 512, 512], replicated, may hold values from -0.25 to 0.25
- proc_msg_out: bfloat16 [2, 512, 512], replicated, may hold values from -0.25 to 0.25
- proc_upd_in: bfloat16 [2, 1024, 512], replicated, may hold values from -0.1875 to 0.1875
- proc_upd_out: bfloat16 [2, 512, 512], replicated, may hold values from -0.25 to 0.25
- proc_gain: float32 [2, 512], replicated, may hold values from 0.1 to 1.9
Outputs:
- mesh_out: bfloat16 [131072, 512], P(('tile', 'dom'))
The draws below stay inside these ranges and needn't reach their ends.
Inputs may be any that keep to these rules, and one draw needn't show every extreme that they name: `g2m_src`: in each row every number from 0 to 159 appears at least once; below 32 it names the device's own grid block, 32 + p the block sent by device p. `g2m_dst`: in each row every mesh block is named by 14 tiles or one more. `m2m_src`: in each row every number from 0 to 31 appears at least once; below 16 it names an own block, then the lower neighbour's rim blocks, then the upper's. `m2m_dst`: in each row every mesh block is named by 7 tiles or one more.
All inputs are finite; a program needn't handle non-finite values.
Results may differ from the reference program's by a relative error of at most 0.018.
Values may be sent and summed in bfloat16 or wider, within the bound.
A program may use at most 128 MiB of HBM per device.

```python
import jax
import jax.numpy as jnp
from jax import lax

D = 512
BLOCK = 64
GB_DEV = 32
MB_DEV = 16
HB = 8
STEPS = 2
ET_G = 224
ET_M = 112
NG = 262144
NM = 131072
N_DOM = 4
DEVICES = 128


def tile_sources(key, row_count, pool_size, tile_count):
    row_keys = jax.random.split(key, row_count)

    def one_row(row_key):
        first_key, second_key, third_key = jax.random.split(row_key, 3)
        covering = jax.random.permutation(first_key, pool_size).astype(jnp.int32)
        repeats = jax.random.randint(second_key, (tile_count - pool_size,), 0, pool_size).astype(jnp.int32)
        return jax.random.permutation(third_key, jnp.concatenate([covering, repeats]))
    return jax.vmap(one_row)(row_keys).astype(jnp.int32)


def tile_targets(key, row_count, blocks, tile_count):
    row_keys = jax.random.split(key, row_count)
    cyclic_ids = jnp.arange(tile_count, dtype=jnp.int32) % blocks
    return jax.vmap(lambda row_key: jax.random.permutation(row_key, cyclic_ids))(row_keys).astype(jnp.int32)


def draw_g2m_src(key, part):
    key = jax.random.fold_in(key, 11)
    return tile_sources(key, DEVICES, GB_DEV + DEVICES, ET_G)


def draw_g2m_dst(key, part):
    key = jax.random.fold_in(key, 12)
    return tile_targets(key, DEVICES, MB_DEV, ET_G)


def draw_m2m_src(key, part):
    key = jax.random.fold_in(key, 13)
    return tile_sources(key, DEVICES, MB_DEV + 2 * HB, ET_M)


def draw_m2m_dst(key, part):
    key = jax.random.fold_in(key, 14)
    return tile_targets(key, DEVICES, MB_DEV, ET_M)


def place_ends(array, key, least, top_value):
    extent = array.shape
    place = [jax.random.randint(jax.random.fold_in(key, axis), (), 0, extent[axis]) for axis in range(len(extent))]
    array = array.at[tuple(place)].set(least)
    longest = extent.index(max(extent))
    place[longest] = (place[longest] + 1) % extent[longest]
    return array.at[tuple(place)].set(top_value)


def steps_of(own_key, dims, cuts, smallest, high):
    level, own = 1.0, jax.random.fold_in(own_key, 6)
    for axis_at, blocks in cuts:
        heights = jnp.exp(jax.random.uniform(jax.random.fold_in(own, axis_at), (blocks,), jnp.float32, smallest / len(cuts), high / len(cuts)))
        level = level * jnp.repeat(heights, dims[axis_at] // blocks).reshape([-1 if axis == axis_at else 1 for axis in range(len(dims))])
    return level


def bell_draw(own_key, shape, deviation, limit, shards=(), kind=jnp.bfloat16):
    result = deviation * jax.random.normal(own_key, shape, jnp.float32)
    if shards:
        result = result * steps_of(own_key, shape, shards, -0.22, 0.18)
    return jnp.clip(result, -limit, limit).astype(kind)


def setup_inputs(seed: int = 0) -> dict:
    key_of = jax.random.split(jax.random.key(seed), 21)
    grid_latent = bell_draw(key_of[0], (NG, D), 1.0, 6.0, ((0, 128),))
    mesh_latent = bell_draw(key_of[1], (NM, D), 1.0, 6.0, ((0, 128),))
    g2m_send = place_ends(jax.random.randint(key_of[2], (DEVICES, DEVICES), 0, GB_DEV), jax.random.fold_in(key_of[2], 1), 0, GB_DEV - 1).astype(jnp.int32)
    g2m_src = draw_g2m_src(jax.random.fold_in(key_of[20], 71), 0)
    g2m_dst = draw_g2m_dst(jax.random.fold_in(key_of[20], 71), 0)
    g2m_weight = bell_draw(key_of[5], (DEVICES * ET_G, BLOCK, BLOCK), (BLOCK * ET_G // MB_DEV) ** -0.5, 0.1875, ((0, 128),))
    halo_send = place_ends(jax.random.randint(key_of[6], (DEVICES, HB), 0, MB_DEV), jax.random.fold_in(key_of[6], 1), 0, MB_DEV - 1).astype(jnp.int32)
    m2m_src = draw_m2m_src(jax.random.fold_in(key_of[20], 71), 0)
    m2m_dst = draw_m2m_dst(jax.random.fold_in(key_of[20], 71), 0)
    m2m_weight = bell_draw(key_of[9], (STEPS, DEVICES * ET_M, BLOCK, BLOCK), (BLOCK * ET_M // MB_DEV) ** -0.5, 0.25, ((1, 128),))
    enc_msg_in = bell_draw(key_of[10], (D, D), D ** -0.5, 0.25)
    enc_msg_out = bell_draw(key_of[11], (D, D), D ** -0.5, 0.25)
    enc_upd_in = bell_draw(key_of[12], (2 * D, D), (2 * D) ** -0.5, 0.1875)
    enc_upd_out = bell_draw(key_of[13], (D, D), D ** -0.5, 0.25)
    enc_gain = jnp.clip(1.0 + 0.18 * jax.random.normal(key_of[14], (D,), jnp.float32), 0.1, 1.9)
    proc_msg_in = bell_draw(key_of[15], (STEPS, D, D), D ** -0.5, 0.25)
    proc_msg_out = bell_draw(key_of[16], (STEPS, D, D), D ** -0.5, 0.25)
    proc_upd_in = bell_draw(key_of[17], (STEPS, 2 * D, D), (2 * D) ** -0.5, 0.1875)
    proc_upd_out = bell_draw(key_of[18], (STEPS, D, D), D ** -0.5, 0.25)
    proc_gain = jnp.clip(1.0 + 0.18 * jax.random.normal(key_of[19], (STEPS, D), jnp.float32), 0.1, 1.9)
    return dict(grid_latent=grid_latent, mesh_latent=mesh_latent, g2m_send=g2m_send, g2m_src=g2m_src, g2m_dst=g2m_dst, g2m_weight=g2m_weight, halo_send=halo_send, m2m_src=m2m_src, m2m_dst=m2m_dst, m2m_weight=m2m_weight, enc_msg_in=enc_msg_in, enc_msg_out=enc_msg_out, enc_upd_in=enc_upd_in, enc_upd_out=enc_upd_out, enc_gain=enc_gain, proc_msg_in=proc_msg_in, proc_msg_out=proc_msg_out, proc_upd_in=proc_upd_in, proc_upd_out=proc_upd_out, proc_gain=proc_gain)


def two_layer(inputs, w_in, w_out):
    hidden = jax.nn.silu(jnp.dot(inputs, w_in, preferred_element_type=jnp.float32)).astype(jnp.bfloat16)
    return jnp.dot(hidden, w_out, preferred_element_type=jnp.float32).astype(jnp.bfloat16)

def aggregate(source_table, sources, targets, weight, blocks):
    gathered = source_table[sources].astype(jnp.float32)
    contrib = jnp.einsum('tij,tid->tjd', weight.astype(jnp.float32), gathered)
    onehot = (targets[:, None] == jnp.arange(blocks, dtype=jnp.int32)[None, :]).astype(jnp.float32)
    summed = jnp.einsum('tb,tjd->bjd', onehot, contrib, precision=lax.Precision.HIGHEST)
    return summed.astype(jnp.bfloat16)

def update(latent, summed, w_in, w_out, norm_gain):
    features = latent.shape[1]
    pre_sum = jnp.dot(latent, w_in[:features], preferred_element_type=jnp.float32)
    pre_sum = pre_sum + jnp.dot(summed, w_in[features:], preferred_element_type=jnp.float32)
    hidden = jax.nn.silu(pre_sum).astype(jnp.bfloat16)
    output_rows = jnp.dot(hidden, w_out, preferred_element_type=jnp.float32)
    row_mean = lax.optimization_barrier(jnp.mean(output_rows, axis=1, keepdims=True))
    centred = output_rows - row_mean
    row_var = lax.optimization_barrier(jnp.mean(centred * centred, axis=1, keepdims=True))
    normed = centred * lax.rsqrt(row_var + 1e-05) * norm_gain
    return (latent.astype(jnp.float32) + normed).astype(jnp.bfloat16)

def reference(grid_latent, mesh_latent, g2m_send, g2m_src, g2m_dst, g2m_weight, halo_send, m2m_src, m2m_dst, m2m_weight, enc_msg_in, enc_msg_out, enc_upd_in, enc_upd_out, enc_gain, proc_msg_in, proc_msg_out, proc_upd_in, proc_upd_out, proc_gain):
    device_ids = jnp.arange(DEVICES, dtype=jnp.int32)
    grid_msg = two_layer(grid_latent, enc_msg_in, enc_msg_out).reshape(DEVICES, GB_DEV, BLOCK, D)
    mesh_blocks = mesh_latent.reshape(DEVICES, MB_DEV * BLOCK, D)
    tile_weight = g2m_weight.reshape(DEVICES, ET_G, BLOCK, BLOCK)

    def encode(device):
        incoming = grid_msg[device_ids, g2m_send[:, device]]
        source_table = jnp.concatenate([grid_msg[device], incoming], axis=0)
        summed = aggregate(source_table, g2m_src[device], g2m_dst[device], tile_weight[device], MB_DEV)
        return update(mesh_blocks[device], summed.reshape(-1, D), enc_upd_in, enc_upd_out, enc_gain)
    mesh_state = lax.map(encode, device_ids)
    lower_dev = device_ids // N_DOM * N_DOM + (device_ids % N_DOM + N_DOM - 1) % N_DOM
    upper_dev = device_ids // N_DOM * N_DOM + (device_ids % N_DOM + 1) % N_DOM
    for layer_index in range(STEPS):
        proc_msg = two_layer(mesh_state.reshape(-1, D), proc_msg_in[layer_index], proc_msg_out[layer_index]).reshape(DEVICES, MB_DEV, BLOCK, D)
        mesh_weight = m2m_weight[layer_index].reshape(DEVICES, ET_M, BLOCK, BLOCK)
        upd_in = proc_upd_in[layer_index]
        upd_out = proc_upd_out[layer_index]
        upd_gain = proc_gain[layer_index]
        previous = mesh_state

        def process(device):
            from_lower = proc_msg[lower_dev[device]][halo_send[lower_dev[device]]]
            from_upper = proc_msg[upper_dev[device]][halo_send[upper_dev[device]]]
            source_table = jnp.concatenate([proc_msg[device], from_lower, from_upper], axis=0)
            summed = aggregate(source_table, m2m_src[device], m2m_dst[device], mesh_weight[device], MB_DEV)
            return update(previous[device], summed.reshape(-1, D), upd_in, upd_out, upd_gain)
        mesh_state = lax.map(process, device_ids)
    return mesh_state.reshape(-1, D)
```

```python
import functools

import jax
import jax.numpy as jnp
from jax import lax
from jax.experimental import pallas as pl
from jax.experimental.pallas import tpu as pltpu
from jax.sharding import PartitionSpec as P

MESH = pl.DeviceIdType.MESH
F32 = jnp.float32
BF16 = jnp.bfloat16


def silu(v):
    half = 0.5 * v
    return half + half * jnp.tanh(half)


def mm(a, b):
    return jnp.dot(a, b, preferred_element_type=F32)


def pick(table, index):
    hit = index[:, None] == jnp.arange(table.shape[0], dtype=jnp.int32)[None, :]
    return jnp.sum(jnp.where(hit, table[None, :], 0), axis=1)


def invert(place):
    ids = jnp.arange(place.shape[0], dtype=jnp.int32)
    return jnp.sum(jnp.where(place[None, :] == ids[:, None], ids[None, :], 0), axis=1)


def grouped(group):
    count = group.shape[0]
    key = group * count + jnp.arange(count, dtype=jnp.int32)
    rank = jnp.sum((key[None, :] < key[:, None]).astype(jnp.int32), axis=1)
    return invert(rank)


def grid_kernel(send, latent, w_in, w_out, msg, outgoing):
    blocks, rows, width = latent.shape
    step = 4

    def mlp(i, _):
        at = pl.ds(i * step, step)
        x = latent[at].reshape(step * rows, width)
        h = silu(mm(x, w_in[...])).astype(BF16)
        msg[at] = mm(h, w_out[...]).astype(BF16).reshape(step, rows, width)
        return 0

    lax.fori_loop(0, blocks // step, mlp, 0)

    def put(i, _):
        for k in range(4):
            outgoing[i * 4 + k] = msg[send[i * 4 + k]]
        return 0

    lax.fori_loop(0, send.shape[0] // 4, put, 0)


def mesh_kernel(
    g_src, m_src, perm, place, halo_at,
    own, incoming, wt_g, wt_m, latent,
    e_in, e_out, e_gain, m_in, m_out, u_in, u_out, u_gain,
    out, table, state, mine, ptable0, ptable1, payload0, payload1, load_sem, send_sem, recv_sem,
):
    blocks, rows, width = latent.shape
    rim = halo_at.shape[0]
    ptable, payload = (ptable0, ptable1), (payload0, payload1)
    steps = wt_m.shape[0]
    n_dom = lax.axis_size("dom")
    x = lax.axis_index("dom")
    t = lax.axis_index("tile")
    upper = (t, lax.rem(x + 1, n_dom))
    lower = (t, lax.rem(x + n_dom - 1, n_dom))
    quarter = blocks // 4
    half_rim = rim // 2

    barrier = pltpu.get_barrier_semaphore()
    for peer in (lower, upper):
        pl.semaphore_signal(barrier, inc=1, device_id=peer, device_id_type=MESH)
    loads = [
        pltpu.make_async_copy(own, table.at[pl.ds(0, own.shape[0])], load_sem.at[0]),
        pltpu.make_async_copy(incoming, table.at[pl.ds(own.shape[0], incoming.shape[0])], load_sem.at[1]),
    ]
    for c in loads:
        c.start()
    pl.semaphore_wait(barrier, 2)
    for c in loads:
        c.wait()

    def halo(s, h):
        src = payload[s].at[pl.ds(h * half_rim, half_rim)]
        up = pltpu.make_async_remote_copy(
            src, ptable[s].at[pl.ds(blocks + h * half_rim, half_rim)],
            send_sem.at[s, 0, h], recv_sem.at[s, 0, h], device_id=upper, device_id_type=MESH)
        down = pltpu.make_async_remote_copy(
            src, ptable[s].at[pl.ds(blocks + rim + h * half_rim, half_rim)],
            send_sem.at[s, 1, h], recv_sem.at[s, 1, h], device_id=lower, device_id_type=MESH)
        return up, down

    def summed(tab, idx, wt, slots, c):
        parts = []
        for i in range(quarter):
            p = c * quarter + i
            got = jnp.concatenate([tab[idx[p * slots + k]] for k in range(slots)], axis=0)
            parts.append(mm(wt[p], got).astype(BF16))
        return jnp.concatenate(parts, axis=0)

    def update(old, agg, w_in, w_out, gain):
        pre = mm(old, w_in[pl.ds(0, width), :]) + mm(agg, w_in[pl.ds(width, width), :])
        o = mm(silu(pre).astype(BF16), w_out[...])
        mean = jnp.mean(o, axis=1, keepdims=True)
        cen = o - mean
        var = jnp.mean(cen * cen, axis=1, keepdims=True)
        normed = cen * lax.rsqrt(var + 1e-05) * gain
        return (old.astype(F32) + normed).astype(BF16)

    def message(s, c, new):
        h = silu(mm(new, m_in[s])).astype(BF16)
        msg = mm(h, m_out[s]).astype(BF16)
        msg = msg.reshape(quarter, rows, width)
        mine[pl.ds(c * quarter, quarter)] = msg
        ptable[s][pl.ds(c * quarter, quarter)] = msg

    def push(s, h):
        for i in range(half_rim):
            payload[s][h * half_rim + i] = mine[halo_at[h * half_rim + i]]
        for c in halo(s, h):
            c.start()

    slots_g = g_src.shape[0] // blocks
    slots_m = m_src.shape[0] // blocks

    def enc_chunk(c):
        agg = summed(table, g_src, wt_g, slots_g, c)
        old = jnp.concatenate([latent[perm[c * quarter + i]] for i in range(quarter)], axis=0)
        new = update(old, agg, e_in, e_out, e_gain[...])
        state[pl.ds(c * quarter, quarter)] = new.reshape(quarter, rows, width)
        message(0, c, new)

    def proc_chunk(s, c):
        agg = summed(ptable[s], m_src, wt_m.at[s], slots_m, c)
        old = state[pl.ds(c * quarter, quarter)].reshape(quarter * rows, width)
        new = update(old, agg, u_in.at[s], u_out.at[s], u_gain[pl.ds(s, 1), :])
        state[pl.ds(c * quarter, quarter)] = new.reshape(quarter, rows, width)
        if s + 1 < steps:
            message(s + 1, c, new)

    def rest(chunk, first):
        def body(c, _):
            chunk(c)
            return 0
        lax.fori_loop(first, 4, body, 0)

    enc_chunk(0)
    push(0, 0)
    enc_chunk(1)
    push(0, 1)
    rest(enc_chunk, 2)
    for s in range(steps):
        for h in range(2):
            for c in halo(s, h):
                c.wait()
        if s + 1 < steps:
            proc_chunk(s, 0)
            push(s + 1, 0)
            proc_chunk(s, 1)
            push(s + 1, 1)
            rest(functools.partial(proc_chunk, s), 2)
        else:
            rest(functools.partial(proc_chunk, s), 0)

    def restore(b, _):
        out[b] = state[place[b]]
        return 0

    lax.fori_loop(0, blocks, restore, 0)


def on_device(
    grid_latent, mesh_latent, g2m_send, g2m_src, g2m_dst, g2m_weight, halo_send, m2m_src, m2m_dst, m2m_weight,
    enc_msg_in, enc_msg_out, enc_upd_in, enc_upd_out, enc_gain,
    proc_msg_in, proc_msg_out, proc_upd_in, proc_upd_out, proc_gain,
):
    rows = g2m_weight.shape[1]
    width = grid_latent.shape[1]
    grid_blocks = grid_latent.shape[0] // rows
    blocks = mesh_latent.shape[0] // rows
    steps = proc_msg_in.shape[0]
    rim = halo_send.shape[1]
    peers = g2m_send.shape[1]
    vmem = pl.BlockSpec(memory_space=pltpu.VMEM)
    smem = pl.BlockSpec(memory_space=pltpu.SMEM)
    hbm = pl.BlockSpec(memory_space=pl.ANY)

    grid_msg, outgoing = pl.pallas_call(
        grid_kernel,
        out_shape=[
            jax.ShapeDtypeStruct((grid_blocks, rows, width), BF16),
            jax.ShapeDtypeStruct((peers, rows, width), BF16),
        ],
        in_specs=[smem, vmem, vmem, vmem],
        out_specs=[vmem, vmem],
        compiler_params=pltpu.CompilerParams(vmem_limit_bytes=32 * 2**20),
        name="grid_messages",
    )(g2m_send[0], grid_latent.reshape(grid_blocks, rows, width), enc_msg_in, enc_msg_out)
    incoming = lax.all_to_all(outgoing, ("tile", "dom"), split_axis=0, concat_axis=0, tiled=True)

    ids = jnp.arange(blocks, dtype=jnp.int32)
    named = halo_send[0][None, :] == ids[:, None]
    first = jnp.min(
        jnp.where(named, jnp.arange(rim, dtype=jnp.int32)[None, :], rim + ids[:, None]), axis=1
    )
    place = jnp.sum((first[None, :] < first[:, None]).astype(jnp.int32), axis=1)
    perm = invert(place)
    halo_at = pick(place, halo_send[0])
    g_order = grouped(pick(place, g2m_dst[0]))
    m_order = grouped(pick(place, m2m_dst[0]))
    g_src = pick(g2m_src[0], g_order)
    m_from = pick(m2m_src[0], m_order)
    m_src = jnp.where(m_from < blocks, pick(place, m_from), m_from)
    wt_g = jnp.transpose(
        g2m_weight[g_order].reshape(blocks, -1, rows, rows), (0, 3, 1, 2)
    ).reshape(blocks, rows, -1)
    wt_m = jnp.transpose(
        m2m_weight[:, m_order].reshape(steps, blocks, -1, rows, rows), (0, 1, 4, 2, 3)
    ).reshape(steps, blocks, rows, -1)

    out = pl.pallas_call(
        mesh_kernel,
        out_shape=jax.ShapeDtypeStruct((blocks, rows, width), BF16),
        in_specs=[smem] * 5 + [hbm, hbm] + [vmem] * 11,
        out_specs=vmem,
        scratch_shapes=[
            pltpu.VMEM((grid_blocks + peers, rows, width), BF16),
            pltpu.VMEM((blocks, rows, width), BF16),
            pltpu.VMEM((blocks, rows, width), BF16),
            pltpu.VMEM((blocks + 2 * rim, rows, width), BF16),
            pltpu.VMEM((blocks + 2 * rim, rows, width), BF16),
            pltpu.VMEM((rim, rows, width), BF16),
            pltpu.VMEM((rim, rows, width), BF16),
            pltpu.SemaphoreType.DMA((2,)),
            pltpu.SemaphoreType.DMA((steps, 2, 2)),
            pltpu.SemaphoreType.DMA((steps, 2, 2)),
        ],
        compiler_params=pltpu.CompilerParams(
            collective_id=0, has_side_effects=True, vmem_limit_bytes=48 * 2**20
        ),
        name="mesh_steps",
    )(
        g_src, m_src, perm, place, halo_at,
        grid_msg, incoming, wt_g, wt_m, mesh_latent.reshape(blocks, rows, width),
        enc_upd_in, enc_upd_out, enc_gain.reshape(1, width),
        proc_msg_in, proc_msg_out, proc_upd_in, proc_upd_out, proc_gain,
    )
    return out.reshape(blocks * rows, width)


def solution(mesh):
    both = P(("tile", "dom"), None)
    whole = P()
    placed = (
        both, both, both, both, both, P(("tile", "dom"), None, None), both, both, both,
        P(None, ("tile", "dom"), None, None),
    ) + (whole,) * 10
    return jax.shard_map(
        on_device, mesh=mesh, in_specs=placed, out_specs=both, check_vma=False
    )
```

```python
import functools

import jax
import jax.numpy as jnp
from jax import lax
from jax.experimental import pallas as pl
from jax.experimental.pallas import tpu as pltpu
from jax.sharding import PartitionSpec as P

MESH = pl.DeviceIdType.MESH
F32 = jnp.float32
BF16 = jnp.bfloat16


def silu(v):
    half = 0.5 * v
    return half + half * jnp.tanh(half)


def mm(a, b):
    return jnp.dot(a, b, preferred_element_type=F32)


def pick(table, index):
    hit = index[:, None] == jnp.arange(table.shape[0], dtype=jnp.int32)[None, :]
    return jnp.sum(jnp.where(hit, table[None, :], 0), axis=1)


def invert(place):
    ids = jnp.arange(place.shape[0], dtype=jnp.int32)
    return jnp.sum(jnp.where(place[None, :] == ids[:, None], ids[None, :], 0), axis=1)


def grouped(group):
    count = group.shape[0]
    key = group * count + jnp.arange(count, dtype=jnp.int32)
    rank = jnp.sum((key[None, :] < key[:, None]).astype(jnp.int32), axis=1)
    return invert(rank)


PARTS = 4
LINES = (("x", "y", "z"), ("y", "z", "x"), ("z", "x", "y"), ("x", "y", "z"))
AXES = ("x", "y", "z")


def whole_kernel(
    g_order, g_src, m_order, m_src, perm, place, halo_at,
    send_row, grid_latent, latent_in, g_weight, m_weight,
    a_in_h, a_out_h, e_in_h, e_out_h, e_gain, m_in_h, m_out_h, u_in_h, u_out_h, u_gain,
    out_h,
    grid_x, a_in, a_out, e_in, e_out, m_in, m_out, u_in, u_out, latent,
    raw, wt_g, wt_m, table, ag0, ag1, ag2, ag3, s0, s1, s2, r0, r1, r2, r3,
    state, mine, ptable0, ptable1, payload0, payload1, own_row, rows_v, rows_s,
    chunk_sem, load_sem, row_s, row_r, ag_s, ag_r, relay_s, relay_r, mid_s, mid_r, last_s, last_r, local_sem,
    send_sem, recv_sem,
):
    blocks, rows, width = latent.shape
    grid_blocks = grid_x.shape[0]
    sub = rows // PARTS
    rim = halo_at.shape[0]
    steps = m_in.shape[0]
    ptable, payload = (ptable0, ptable1), (payload0, payload1)
    ag, stage, held = (ag0, ag1, ag2, ag3), (s0, s1, s2, s0), (r0, r1, r2, r3)
    tile = lax.axis_index("tile")
    core = lax.rem(tile, 2)
    at = {"x": lax.axis_index("dom"), "y": lax.rem(tile // 2, 4), "z": tile // 8}

    def device(c, core_at):
        return (c["z"] * 4 + c["y"]) * 2 + core_at, c["x"]

    def moved(axis, by, flip=0):
        c = dict(at)
        c[axis] = lax.rem(at[axis] + by + 4, 4)
        return device(c, lax.rem(core + flip, 2))

    chunk = 4
    chunks = grid_blocks // chunk

    def chunk_load(i):
        return pltpu.make_async_copy(
            grid_latent.at[pl.ds(i * chunk, chunk)], grid_x.at[pl.ds(i * chunk, chunk)], chunk_sem.at[i])

    loads = [
        pltpu.make_async_copy(src, dst, load_sem.at[i])
        for i, (src, dst) in enumerate((
            (a_in_h, a_in), (a_out_h, a_out), (send_row, own_row), (g_weight, raw), (latent_in, latent),
            (e_in_h, e_in), (e_out_h, e_out), (m_in_h, m_in), (m_out_h, m_out), (u_in_h, u_in), (u_out_h, u_out),
        ))
    ]
    loads[0].start()
    chunk_load(0).start()
    loads[1].start()
    loads[2].start()
    for i in range(1, chunks):
        chunk_load(i).start()
    for c in loads[3:]:
        c.start()

    barrier = pltpu.get_barrier_semaphore()
    greeted = [moved(axis, by, flip) for axis in AXES for by in (1, 2, 3) for flip in (0, 1)] + [moved("x", 0, 1)]
    for peer in greeted:
        pl.semaphore_signal(barrier, inc=1, device_id=peer, device_id_type=MESH)

    def mlp(i, _):
        chunk_load(i).wait()
        x = grid_x[pl.ds(i * chunk, chunk)].reshape(chunk * rows, width)
        h = silu(mm(x, a_in[...])).astype(BF16)
        msg = mm(h, a_out[...]).astype(BF16).reshape(chunk, rows, width)
        table[0, i // 2, lax.rem(i, 2)] = msg
        for p in range(PARTS):
            ag[p][at[LINES[p][0]], pl.ds(i * chunk, chunk)] = msg[:, p * sub:(p + 1) * sub]
        return 0

    half = grid_blocks // 2

    def gather_copy(p, way, h):
        axis = LINES[p][0]
        ref = ag[p].at[at[axis], pl.ds(h * half, half)]
        return pltpu.make_async_remote_copy(
            ref, ref, ag_s.at[p, way, h], ag_r.at[p, way, h],
            device_id=moved(axis, 1 - 2 * way), device_id_type=MESH)

    def relay_copy(p, way):
        axis = LINES[p][0]
        by = 1 - 2 * way
        ref = ag[p].at[lax.rem(at[axis] - by + 4, 4), pl.ds(way * half, half)]
        return pltpu.make_async_remote_copy(
            ref, ref, relay_s.at[p, way], relay_r.at[p, way],
            device_id=moved(axis, by), device_id_type=MESH)

    def row_copy(a, by):
        axis = AXES[a]
        return pltpu.make_async_remote_copy(
            own_row, rows_v.at[a, at[axis]], row_s.at[a, by - 1], row_r.at[a, by - 1],
            device_id=moved(axis, by), device_id_type=MESH)

    loads[0].wait()
    loads[1].wait()
    lax.fori_loop(0, chunks // 2, mlp, 0)
    pl.semaphore_wait(barrier, len(greeted))
    for p in range(3):
        for way in (0, 1):
            gather_copy(p, way, 0).start()
    loads[2].wait()
    for a in range(3):
        for by in (1, 2, 3):
            row_copy(a, by).start()
    own_rows = [pltpu.make_async_copy(own_row, rows_v.at[a, at[AXES[a]]], local_sem.at[a]) for a in range(3)]
    for c in own_rows:
        c.start()
    lax.fori_loop(chunks // 2, chunks, mlp, 0)
    for p in range(3):
        for way in (0, 1):
            gather_copy(p, way, 1).start()

    def relays(p):
        for way in (0, 1):
            gather_copy(p, way, way).wait_recv()
            relay_copy(p, way).start()

    def gathered(p):
        for way in (0, 1):
            gather_copy(p, way, 1 - way).wait_recv()
            relay_copy(p, way).wait_recv()

    def held_at(p, b):
        return held[p].at[:, b] if p == 2 else held[p].at[b]

    def mid_copy(p, by):
        axis = LINES[p][1]
        return pltpu.make_async_remote_copy(
            stage[p].at[by - 1], held_at(p, at[axis]), mid_s.at[p, by - 1], mid_r.at[p, by - 1],
            device_id=moved(axis, by), device_id_type=MESH)

    def select(p):
        first, second, third = LINES[p]
        a = AXES.index(first)

        def of(by, j):
            c = dict(at)
            c[second] = lax.rem(at[second] + by, 4)
            for k in range(8):
                c[third] = k // 2
                t, x = device(c, k % 2)
                got = ag[p][j, rows_s[a, j, 0, t * 4 + x]]
                yield k // 2, k % 2, got

        def keep(j, _):
            for c3, k, got in of(0, j):
                if p == 2:
                    held[p][j, at[second], c3, k] = got
                else:
                    held[p][at[second], j, c3, k] = got
            return 0

        def put(i, _):
            by, j = 1 + i // 4, lax.rem(i, 4)
            for c3, k, got in of(by, j):
                stage[p][by - 1, j, c3, k] = got
            return 0

        lax.fori_loop(0, 12, put, 0)
        for by in (1, 2, 3):
            mid_copy(p, by).start()
        lax.fori_loop(0, 4, keep, 0)

    def arrived(p):
        for by in (1, 2, 3):
            mid_copy(p, by).wait_recv()

    def landing(p):
        here = pl.ds(p * sub, sub)
        if p == 1:
            return table.at[pl.ds(1, 4), :, core, at["x"], here]
        if p == 2:
            return table.at[pl.ds(1, 4), at["y"], core, :, here]
        return table.at[1 + at["z"], :, core, :, here]

    others = [(by, flip) for by in (1, 3, 2, 0) for flip in (0, 1) if by or flip]

    def last_copy(p, by, flip):
        axis = LINES[p][2]
        return pltpu.make_async_remote_copy(
            held[p].at[:, :, lax.rem(at[axis] + by, 4), lax.rem(core + flip, 2)], landing(p),
            last_s.at[p, by, flip], last_r.at[p, by, flip],
            device_id=moved(axis, by, flip), device_id_type=MESH)

    def keep_copy(p):
        return pltpu.make_async_copy(held[p].at[:, :, at[LINES[p][2]], core], landing(p), local_sem.at[3 + p])

    def deliver(p):
        for by, flip in others:
            last_copy(p, by, flip).start()
        keep_copy(p).start()

    slots_g = g_src.shape[0] // blocks
    slots_m = m_src.shape[0] // blocks

    def prepare(order, base, wt, slots):
        def body(b, _):
            cat = jnp.concatenate([raw[base + order[b * slots + k]] for k in range(slots)], axis=0)
            wt[b] = cat.T
            return 0
        lax.fori_loop(0, blocks, body, 0)

    for p in range(3):
        relays(p)
    for a in range(3):
        own_rows[a].wait()
        for by in (1, 2, 3):
            row_copy(a, by).wait()
    to_scalar = pltpu.make_async_copy(rows_v, rows_s, local_sem.at[0])
    to_scalar.start()
    to_scalar.wait()

    gathered(0)
    for h in (0, 1):
        for way in (0, 1):
            gather_copy(3, way, h).start()
    select(0)
    gathered(1)
    select(1)
    gathered(2)
    loads[3].wait()
    prepare(g_order, 0, wt_g, slots_g)
    m_load = pltpu.make_async_copy(m_weight, raw, load_sem.at[3])
    m_load.start()
    relays(3)
    gathered(3)
    select(2)
    arrived(0)
    for by in (1, 2, 3):
        mid_copy(0, by).wait_send()
    select(3)
    deliver(0)
    m_load.wait()
    for s in range(steps):
        prepare(m_order, s * (raw.shape[0] // steps), wt_m.at[s], slots_m)
    arrived(1)
    arrived(2)
    deliver(1)
    deliver(2)
    arrived(3)
    deliver(3)
    for c in loads[4:]:
        c.wait()
    for p in range(PARTS):
        for by, flip in others:
            last_copy(p, by, flip).wait_recv()
        keep_copy(p).wait()

    n_dom = lax.axis_size("dom")
    upper, lower = moved("x", 1), moved("x", 3)
    quarter = blocks // 4
    half_rim = rim // 2

    def halo(s, h):
        src = payload[s].at[pl.ds(h * half_rim, half_rim)]
        up = pltpu.make_async_remote_copy(
            src, ptable[s].at[pl.ds(blocks + h * half_rim, half_rim)],
            send_sem.at[s, 0, h], recv_sem.at[s, 0, h], device_id=upper, device_id_type=MESH)
        down = pltpu.make_async_remote_copy(
            src, ptable[s].at[pl.ds(blocks + rim + h * half_rim, half_rim)],
            send_sem.at[s, 1, h], recv_sem.at[s, 1, h], device_id=lower, device_id_type=MESH)
        return up, down

    def from_grid(i):
        return table[i // 32, lax.rem(i // 8, 4), lax.rem(i // 4, 2), lax.rem(i, 4)]

    def summed(load, idx, wt, slots, c):
        parts = []
        for i in range(quarter):
            p = c * quarter + i
            got = jnp.concatenate([load(idx[p * slots + k]) for k in range(slots)], axis=0)
            parts.append(mm(wt[p], got).astype(BF16))
        return jnp.concatenate(parts, axis=0)

    def update(old, agg, w_in, w_out, gain):
        pre = mm(old, w_in[pl.ds(0, width), :]) + mm(agg, w_in[pl.ds(width, width), :])
        o = mm(silu(pre).astype(BF16), w_out[...])
        mean = jnp.mean(o, axis=1, keepdims=True)
        cen = o - mean
        var = jnp.mean(cen * cen, axis=1, keepdims=True)
        normed = cen * lax.rsqrt(var + 1e-05) * gain
        return (old.astype(F32) + normed).astype(BF16)

    def message(s, c, new):
        h = silu(mm(new, m_in[s])).astype(BF16)
        msg = mm(h, m_out[s]).astype(BF16)
        msg = msg.reshape(quarter, rows, width)
        mine[pl.ds(c * quarter, quarter)] = msg
        ptable[s][pl.ds(c * quarter, quarter)] = msg

    def push(s, h):
        for i in range(half_rim):
            payload[s][h * half_rim + i] = mine[halo_at[h * half_rim + i]]
        for c in halo(s, h):
            c.start()

    def enc_chunk(c):
        agg = summed(from_grid, g_src, wt_g, slots_g, c)
        old = jnp.concatenate([latent[perm[c * quarter + i]] for i in range(quarter)], axis=0)
        new = update(old, agg, e_in, e_out, e_gain[...])
        state[pl.ds(c * quarter, quarter)] = new.reshape(quarter, rows, width)
        message(0, c, new)

    def proc_chunk(s, c):
        agg = summed(lambda i: ptable[s][i], m_src, wt_m.at[s], slots_m, c)
        old = state[pl.ds(c * quarter, quarter)].reshape(quarter * rows, width)
        new = update(old, agg, u_in.at[s], u_out.at[s], u_gain[pl.ds(s, 1), :])
        state[pl.ds(c * quarter, quarter)] = new.reshape(quarter, rows, width)
        if s + 1 < steps:
            message(s + 1, c, new)

    def rest(chunk, first):
        def body(c, _):
            chunk(c)
            return 0
        lax.fori_loop(first, 4, body, 0)

    enc_chunk(0)
    push(0, 0)
    enc_chunk(1)
    push(0, 1)
    rest(enc_chunk, 2)
    for s in range(steps):
        for h in range(2):
            for c in halo(s, h):
                c.wait()
        if s + 1 < steps:
            proc_chunk(s, 0)
            push(s + 1, 0)
            proc_chunk(s, 1)
            push(s + 1, 1)
            rest(functools.partial(proc_chunk, s), 2)
        else:
            rest(functools.partial(proc_chunk, s), 0)

    def restore(b, _):
        mine[b] = state[place[b]]
        return 0

    lax.fori_loop(0, blocks, restore, 0)
    store = pltpu.make_async_copy(mine, out_h, local_sem.at[0])
    store.start()
    for p in range(PARTS):
        for way in (0, 1):
            relay_copy(p, way).wait_send()
            for h in (0, 1):
                gather_copy(p, way, h).wait_send()
        for by, flip in others:
            last_copy(p, by, flip).wait_send()
        if p:
            for by in (1, 2, 3):
                mid_copy(p, by).wait_send()
    store.wait()


def on_device(
    grid_latent, mesh_latent, g2m_send, g2m_src, g2m_dst, g2m_weight, halo_send, m2m_src, m2m_dst, m2m_weight,
    enc_msg_in, enc_msg_out, enc_upd_in, enc_upd_out, enc_gain,
    proc_msg_in, proc_msg_out, proc_upd_in, proc_upd_out, proc_gain,
):
    rows = g2m_weight.shape[1]
    width = grid_latent.shape[1]
    grid_blocks = grid_latent.shape[0] // rows
    blocks = mesh_latent.shape[0] // rows
    steps = proc_msg_in.shape[0]
    rim = halo_send.shape[1]
    peers = g2m_send.shape[1]
    vmem = pl.BlockSpec(memory_space=pltpu.VMEM)
    smem = pl.BlockSpec(memory_space=pltpu.SMEM)
    hbm = pl.BlockSpec(memory_space=pl.ANY)

    ids = jnp.arange(blocks, dtype=jnp.int32)
    named = halo_send[0][None, :] == ids[:, None]
    first = jnp.min(
        jnp.where(named, jnp.arange(rim, dtype=jnp.int32)[None, :], rim + ids[:, None]), axis=1
    )
    place = jnp.sum((first[None, :] < first[:, None]).astype(jnp.int32), axis=1)
    perm = invert(place)
    halo_at = pick(place, halo_send[0])
    g_order = grouped(pick(place, g2m_dst[0]))
    m_order = grouped(pick(place, m2m_dst[0]))
    g_src = pick(g2m_src[0], g_order)
    m_from = pick(m2m_src[0], m_order)
    m_src = jnp.where(m_from < blocks, pick(place, m_from), m_from)
    sub = rows // PARTS
    flying = (4, grid_blocks, sub, width)
    staged = (3, 4, 4, 2, sub, width)
    holding = (4, 4, 4, 2, sub, width)
    dma = pltpu.SemaphoreType.DMA
    vm = pltpu.VMEM
    out = pl.pallas_call(
        whole_kernel,
        out_shape=jax.ShapeDtypeStruct((blocks, rows, width), BF16),
        in_specs=[smem] * 7 + [hbm] * 9 + [vmem] + [hbm] * 4 + [vmem],
        out_specs=hbm,
        scratch_shapes=[
            vm((grid_blocks, rows, width), BF16),
            *[vm(w.shape, BF16) for w in (
                enc_msg_in, enc_msg_out, enc_upd_in, enc_upd_out,
                proc_msg_in, proc_msg_out, proc_upd_in, proc_upd_out)],
            vm((blocks, rows, width), BF16),
            vm(g2m_weight.shape, BF16),
            vm((blocks, rows, rows * (g2m_dst.shape[1] // blocks)), BF16),
            vm((steps, blocks, rows, rows * (m2m_dst.shape[1] // blocks)), BF16),
            vm((5, 4, 2, 4, rows, width), BF16),
            *[vm(flying, BF16)] * 4,
            *[vm(staged, BF16)] * 3,
            *[vm(holding, BF16)] * 4,
            vm((blocks, rows, width), BF16),
            vm((blocks, rows, width), BF16),
            vm((blocks + 2 * rim, rows, width), BF16),
            vm((blocks + 2 * rim, rows, width), BF16),
            vm((rim, rows, width), BF16),
            vm((rim, rows, width), BF16),
            vm((1, peers), jnp.int32),
            vm((3, 4, 1, peers), jnp.int32),
            pltpu.SMEM((3, 4, 1, peers), jnp.int32),
            dma((8,)), dma((11,)), dma((3, 3)), dma((3, 3)),
            dma((4, 2, 2)), dma((4, 2, 2)), dma((4, 2)), dma((4, 2)),
            dma((4, 3)), dma((4, 3)), dma((4, 4, 2)), dma((4, 4, 2)), dma((7,)),
            dma((steps, 2, 2)), dma((steps, 2, 2)),
        ],
        compiler_params=pltpu.CompilerParams(
            collective_id=0, has_side_effects=True, vmem_limit_bytes=62 * 2**20
        ),
        name="encoder_and_steps",
    )(
        g_order, g_src, m_order, m_src, perm, place, halo_at,
        g2m_send, grid_latent.reshape(grid_blocks, rows, width), mesh_latent.reshape(blocks, rows, width),
        g2m_weight, m2m_weight.reshape(g2m_weight.shape),
        enc_msg_in, enc_msg_out, enc_upd_in, enc_upd_out, enc_gain.reshape(1, width),
        proc_msg_in, proc_msg_out, proc_upd_in, proc_upd_out, proc_gain,
    )
    return out.reshape(blocks * rows, width)


def solution(mesh):
    both = P(("tile", "dom"), None)
    whole = P()
    placed = (
        both, both, both, both, both, P(("tile", "dom"), None, None), both, both, both,
        P(None, ("tile", "dom"), None, None),
    ) + (whole,) * 10
    return jax.shard_map(
        on_device, mesh=mesh, in_specs=placed, out_specs=both, check_vma=False
    )
```

```python
import functools

import jax
import jax.numpy as jnp
from jax import lax
from jax.experimental import pallas as pl
from jax.experimental.pallas import tpu as pltpu
from jax.sharding import PartitionSpec as P

MESH = pl.DeviceIdType.MESH
F32 = jnp.float32
BF16 = jnp.bfloat16


def silu(v):
    half = 0.5 * v
    return half + half * jnp.tanh(half)


def mm(a, b):
    return jnp.dot(a, b, preferred_element_type=F32)


def iota(shape, dim):
    return lax.broadcasted_iota(jnp.int32, shape, dim)


def total(mask, values, axis):
    return jnp.sum(jnp.where(mask, values, 0), axis=axis, keepdims=True)


def column(row):
    n = row.shape[1]
    return total(iota((n, n), 0) == iota((n, n), 1), row, 1)


def ranks(row):
    n = row.shape[1]
    key = row * n + iota((1, n), 1)
    return total(key < column(key), 1, 1)


def sort_by(rank, col):
    n = col.shape[0]
    return total(rank == iota((n, n), 1), col, 0)


def placed(place, row):
    n = place.shape[0]
    return total(iota((n, row.shape[1]), 0) == row, place, 0)


PARTS = 4
LINES = (("x", "y", "z"), ("y", "z", "x"), ("z", "x", "y"), ("x", "y", "z"))
AXES = ("x", "y", "z")


def whole_kernel(
    g_src_h, g_dst_h, m_src_h, m_dst_h, halo_h,
    send_row, grid_latent, latent_in, g_weight, m_weight,
    a_in_h, a_out_h, e_in_h, e_out_h, e_gain_h, m_in_h, m_out_h, u_in_h, u_out_h, u_gain_h,
    out_h,
    grid_x, a_in, a_out, e_in, e_out, m_in, m_out, u_in, u_out, e_gain, u_gain, latent,
    g_from, g_to, m_from, m_to, halo_of, index_v, index_s,
    lanes_g, lanes_m, raw, wt_g, wt_m, table, ag0, ag1, ag2, ag3, s0, s1, s2, r0, r1, r2, r3,
    state, mine, ptable0, ptable1, payload0, payload1, own_row, rows_v, rows_s,
    chunk_sem, load_sem, row_s, row_r, ag_s, ag_r, relay_s, relay_r, mid_s, mid_r, last_s, last_r, local_sem,
    send_sem, recv_sem,
):
    blocks, rows, width = latent.shape
    grid_blocks = grid_x.shape[0]
    sub = rows // PARTS
    rim = halo_of.shape[1]
    steps = m_in.shape[0]
    ptable, payload = (ptable0, ptable1), (payload0, payload1)
    ag, stage, held = (ag0, ag1, ag2, ag3), (s0, s1, s2, s0), (r0, r1, r2, r3)
    tile = lax.axis_index("tile")
    core = lax.rem(tile, 2)
    at = {"x": lax.axis_index("dom"), "y": lax.rem(tile // 2, 4), "z": tile // 8}

    def device(c, core_at):
        return (c["z"] * 4 + c["y"]) * 2 + core_at, c["x"]

    def moved(axis, by, flip=0):
        c = dict(at)
        c[axis] = lax.rem(at[axis] + by + 4, 4)
        return device(c, lax.rem(core + flip, 2))

    chunk = 4
    chunks = grid_blocks // chunk

    def chunk_load(i):
        return pltpu.make_async_copy(
            grid_latent.at[pl.ds(i * chunk, chunk)], grid_x.at[pl.ds(i * chunk, chunk)], chunk_sem.at[i])

    loads = [
        pltpu.make_async_copy(src, dst, load_sem.at[i])
        for i, (src, dst) in enumerate((
            (a_in_h, a_in), (a_out_h, a_out), (send_row, own_row),
            (g_src_h, g_from), (g_dst_h, g_to), (m_src_h, m_from), (m_dst_h, m_to), (halo_h, halo_of),
            (g_weight, lanes_g), (m_weight, lanes_m), (latent_in, latent), (e_gain_h, e_gain), (u_gain_h, u_gain),
            (e_in_h, e_in), (e_out_h, e_out), (m_in_h, m_in), (m_out_h, m_out), (u_in_h, u_in), (u_out_h, u_out),
        ))
    ]
    loads[0].start()
    chunk_load(0).start()
    loads[1].start()
    loads[2].start()
    for i in range(1, chunks):
        chunk_load(i).start()
    for c in loads[3:]:
        c.start()

    barrier = pltpu.get_barrier_semaphore()
    greeted = [moved(axis, by, flip) for axis in AXES for by in (1, 2, 3) for flip in (0, 1)] + [moved("x", 0, 1)]
    for peer in greeted:
        pl.semaphore_signal(barrier, inc=1, device_id=peer, device_id_type=MESH)

    def mlp(i, _):
        chunk_load(i).wait()
        x = grid_x[pl.ds(i * chunk, chunk)].reshape(chunk * rows, width)
        h = silu(mm(x, a_in[...])).astype(BF16)
        msg = mm(h, a_out[...]).astype(BF16).reshape(chunk, rows, width)
        table[0, i // 2, lax.rem(i, 2)] = msg
        for p in range(PARTS):
            ag[p][at[LINES[p][0]], pl.ds(i * chunk, chunk)] = msg[:, p * sub:(p + 1) * sub]
        return 0

    half = grid_blocks // 2

    def gather_copy(p, way, h):
        axis = LINES[p][0]
        ref = ag[p].at[at[axis], pl.ds(h * half, half)]
        return pltpu.make_async_remote_copy(
            ref, ref, ag_s.at[p, way, h], ag_r.at[p, way, h],
            device_id=moved(axis, 1 - 2 * way), device_id_type=MESH)

    def relay_copy(p, way):
        axis = LINES[p][0]
        by = 1 - 2 * way
        ref = ag[p].at[lax.rem(at[axis] - by + 4, 4), pl.ds(way * half, half)]
        return pltpu.make_async_remote_copy(
            ref, ref, relay_s.at[p, way], relay_r.at[p, way],
            device_id=moved(axis, by), device_id_type=MESH)

    def row_copy(a, by):
        axis = AXES[a]
        return pltpu.make_async_remote_copy(
            own_row, rows_v.at[a, at[axis]], row_s.at[a, by - 1], row_r.at[a, by - 1],
            device_id=moved(axis, by), device_id_type=MESH)

    loads[0].wait()
    loads[1].wait()
    lax.fori_loop(0, chunks // 2, mlp, 0)
    pl.semaphore_wait(barrier, len(greeted))
    for p in range(3):
        for way in (0, 1):
            gather_copy(p, way, 0).start()
    loads[2].wait()
    for a in range(3):
        for by in (1, 2, 3):
            row_copy(a, by).start()
    own_rows = [pltpu.make_async_copy(own_row, rows_v.at[a, at[AXES[a]]], local_sem.at[a]) for a in range(3)]
    for c in own_rows:
        c.start()
    lax.fori_loop(chunks // 2, chunks, mlp, 0)
    for p in range(3):
        for way in (0, 1):
            gather_copy(p, way, 1).start()

    def relays(p):
        for way in (0, 1):
            gather_copy(p, way, way).wait_recv()
            relay_copy(p, way).start()

    def gathered(p):
        for way in (0, 1):
            gather_copy(p, way, 1 - way).wait_recv()
            relay_copy(p, way).wait_recv()

    def held_at(p, b):
        return held[p].at[:, b] if p == 2 else held[p].at[b]

    def mid_copy(p, by):
        axis = LINES[p][1]
        return pltpu.make_async_remote_copy(
            stage[p].at[by - 1], held_at(p, at[axis]), mid_s.at[p, by - 1], mid_r.at[p, by - 1],
            device_id=moved(axis, by), device_id_type=MESH)

    def select(p):
        first, second, third = LINES[p]
        a = AXES.index(first)

        def of(by, j):
            c = dict(at)
            c[second] = lax.rem(at[second] + by, 4)
            for k in range(8):
                c[third] = k // 2
                t, x = device(c, k % 2)
                got = ag[p][j, rows_s[a, j, 0, t * 4 + x]]
                yield k // 2, k % 2, got

        def keep(j, _):
            for c3, k, got in of(0, j):
                if p == 2:
                    held[p][j, at[second], c3, k] = got
                else:
                    held[p][at[second], j, c3, k] = got
            return 0

        def put(i, _):
            by, j = 1 + i // 4, lax.rem(i, 4)
            for c3, k, got in of(by, j):
                stage[p][by - 1, j, c3, k] = got
            return 0

        lax.fori_loop(0, 12, put, 0)
        for by in (1, 2, 3):
            mid_copy(p, by).start()
        lax.fori_loop(0, 4, keep, 0)

    def arrived(p):
        for by in (1, 2, 3):
            mid_copy(p, by).wait_recv()

    def landing(p):
        here = pl.ds(p * sub, sub)
        if p == 1:
            return table.at[pl.ds(1, 4), :, core, at["x"], here]
        if p == 2:
            return table.at[pl.ds(1, 4), at["y"], core, :, here]
        return table.at[1 + at["z"], :, core, :, here]

    others = [(by, flip) for by in (1, 3, 2, 0) for flip in (0, 1) if by or flip]

    def last_copy(p, by, flip):
        axis = LINES[p][2]
        return pltpu.make_async_remote_copy(
            held[p].at[:, :, lax.rem(at[axis] + by, 4), lax.rem(core + flip, 2)], landing(p),
            last_s.at[p, by, flip], last_r.at[p, by, flip],
            device_id=moved(axis, by, flip), device_id_type=MESH)

    def keep_copy(p):
        return pltpu.make_async_copy(held[p].at[:, :, at[LINES[p][2]], core], landing(p), local_sem.at[3 + p])

    def deliver(p):
        for by, flip in others:
            last_copy(p, by, flip).start()
        keep_copy(p).start()

    slots_g = g_to.shape[1] // blocks
    slots_m = m_to.shape[1] // blocks
    packed = 16

    def listed(r, n=1):
        return lambda k: index_s[r, k]

    g_order, g_src, m_order, m_src, perm, place, halo_at = [listed(r) for r in range(7)]

    def index_lists():
        halo_row = halo_of[...]
        named = iota((blocks, rim), 0) == halo_row
        first = jnp.min(
            jnp.where(named, iota((blocks, rim), 1), rim + iota((blocks, rim), 0)), axis=1, keepdims=True)
        first_row = total(iota((blocks, blocks), 0) == iota((blocks, blocks), 1), first, 0)
        spot = total(first_row < first, 1, 1)
        rank_g = ranks(placed(spot, g_to[...]))
        rank_m = ranks(placed(spot, m_to[...]))
        m_row = m_from[...]
        own = jnp.where(m_row < blocks, placed(spot, jnp.minimum(m_row, blocks - 1)), m_row)
        ng, nm = g_to.shape[1], m_to.shape[1]
        for r, row in enumerate((
            sort_by(rank_g, iota((ng, 1), 0)), sort_by(rank_g, column(g_from[...])),
            sort_by(rank_m, iota((nm, 1), 0)), sort_by(rank_m, column(own)),
            sort_by(spot, iota((blocks, 1), 0)),
            total(iota((blocks, blocks), 0) == iota((blocks, blocks), 1), spot, 0),
            placed(spot, halo_row),
        )):
            index_v[pl.ds(r, 1), pl.ds(0, row.shape[1])] = row
        copy = pltpu.make_async_copy(index_v, index_s, local_sem.at[7])
        copy.start()
        return copy

    def unpack(lanes, base, first, last):
        def body(q, _):
            x = lanes[pl.ds(q * packed, packed)]
            tiles = jnp.swapaxes(jnp.swapaxes(x, 1, 2), 0, 1)
            raw[pl.ds(base, tiles.shape[0]), pl.ds(q * packed, packed)] = tiles
            return 0
        lax.fori_loop(first, last, body, 0)

    def prepare(order, base, wt, slots):
        def body(b, _):
            cat = jnp.concatenate([raw[base + order(b * slots + k)] for k in range(slots)], axis=0)
            wt[b] = cat.T
            return 0
        lax.fori_loop(0, blocks, body, 0)

    groups = rows // packed
    for c in loads[3:8]:
        c.wait()
    lists = index_lists()
    loads[8].wait()
    unpack(lanes_g, 0, 0, 2)
    for p in range(3):
        relays(p)
    unpack(lanes_g, 0, 2, groups)
    for a in range(3):
        own_rows[a].wait()
        for by in (1, 2, 3):
            row_copy(a, by).wait()
    to_scalar = pltpu.make_async_copy(rows_v, rows_s, local_sem.at[0])
    to_scalar.start()
    to_scalar.wait()
    lists.wait()

    gathered(0)
    for h in (0, 1):
        for way in (0, 1):
            gather_copy(3, way, h).start()
    select(0)
    gathered(1)
    select(1)
    gathered(2)
    prepare(g_order, 0, wt_g, slots_g)
    relays(3)
    loads[9].wait()
    half_tiles = raw.shape[0] // steps
    unpack(lanes_m.at[0], 0, 0, groups)
    gathered(3)
    select(2)
    unpack(lanes_m.at[1], half_tiles, 0, groups)
    arrived(0)
    for by in (1, 2, 3):
        mid_copy(0, by).wait_send()
    select(3)
    deliver(0)
    for s in range(steps):
        prepare(m_order, s * half_tiles, wt_m.at[s], slots_m)
    arrived(1)
    arrived(2)
    deliver(1)
    deliver(2)
    arrived(3)
    deliver(3)
    for c in loads[10:]:
        c.wait()
    for p in range(PARTS):
        for by, flip in others:
            last_copy(p, by, flip).wait_recv()
        keep_copy(p).wait()

    n_dom = lax.axis_size("dom")
    upper, lower = moved("x", 1), moved("x", 3)
    quarter = blocks // 4
    half_rim = rim // 2

    def halo(s, h):
        src = payload[s].at[pl.ds(h * half_rim, half_rim)]
        up = pltpu.make_async_remote_copy(
            src, ptable[s].at[pl.ds(blocks + h * half_rim, half_rim)],
            send_sem.at[s, 0, h], recv_sem.at[s, 0, h], device_id=upper, device_id_type=MESH)
        down = pltpu.make_async_remote_copy(
            src, ptable[s].at[pl.ds(blocks + rim + h * half_rim, half_rim)],
            send_sem.at[s, 1, h], recv_sem.at[s, 1, h], device_id=lower, device_id_type=MESH)
        return up, down

    def from_grid(i):
        return table[i // 32, lax.rem(i // 8, 4), lax.rem(i // 4, 2), lax.rem(i, 4)]

    def summed(load, idx, wt, slots, c):
        parts = []
        for i in range(quarter):
            p = c * quarter + i
            got = jnp.concatenate([load(idx(p * slots + k)) for k in range(slots)], axis=0)
            parts.append(mm(wt[p], got).astype(BF16))
        return jnp.concatenate(parts, axis=0)

    def update(old, agg, w_in, w_out, gain):
        pre = mm(old, w_in[pl.ds(0, width), :]) + mm(agg, w_in[pl.ds(width, width), :])
        o = mm(silu(pre).astype(BF16), w_out[...])
        mean = jnp.mean(o, axis=1, keepdims=True)
        cen = o - mean
        var = jnp.mean(cen * cen, axis=1, keepdims=True)
        normed = cen * lax.rsqrt(var + 1e-05) * gain
        return (old.astype(F32) + normed).astype(BF16)

    def message(s, c, new):
        h = silu(mm(new, m_in[s])).astype(BF16)
        msg = mm(h, m_out[s]).astype(BF16)
        msg = msg.reshape(quarter, rows, width)
        mine[pl.ds(c * quarter, quarter)] = msg
        ptable[s][pl.ds(c * quarter, quarter)] = msg

    def push(s, h):
        for i in range(half_rim):
            payload[s][h * half_rim + i] = mine[halo_at(h * half_rim + i)]
        for c in halo(s, h):
            c.start()

    def enc_chunk(c):
        agg = summed(from_grid, g_src, wt_g, slots_g, c)
        old = jnp.concatenate([latent[perm(c * quarter + i)] for i in range(quarter)], axis=0)
        new = update(old, agg, e_in, e_out, e_gain[...])
        state[pl.ds(c * quarter, quarter)] = new.reshape(quarter, rows, width)
        message(0, c, new)

    def proc_chunk(s, c):
        agg = summed(lambda i: ptable[s][i], m_src, wt_m.at[s], slots_m, c)
        old = state[pl.ds(c * quarter, quarter)].reshape(quarter * rows, width)
        new = update(old, agg, u_in.at[s], u_out.at[s], u_gain[pl.ds(s, 1), :])
        state[pl.ds(c * quarter, quarter)] = new.reshape(quarter, rows, width)
        if s + 1 < steps:
            message(s + 1, c, new)

    def rest(chunk, first):
        def body(c, _):
            chunk(c)
            return 0
        lax.fori_loop(first, 4, body, 0)

    enc_chunk(0)
    push(0, 0)
    enc_chunk(1)
    push(0, 1)
    rest(enc_chunk, 2)
    for s in range(steps):
        for h in range(2):
            for c in halo(s, h):
                c.wait()
        if s + 1 < steps:
            proc_chunk(s, 0)
            push(s + 1, 0)
            proc_chunk(s, 1)
            push(s + 1, 1)
            rest(functools.partial(proc_chunk, s), 2)
        else:
            rest(functools.partial(proc_chunk, s), 0)

    def restore(b, _):
        mine[b] = state[place(b)]
        return 0

    lax.fori_loop(0, blocks, restore, 0)
    store = pltpu.make_async_copy(mine, out_h, local_sem.at[0])
    store.start()
    for p in range(PARTS):
        for way in (0, 1):
            relay_copy(p, way).wait_send()
            for h in (0, 1):
                gather_copy(p, way, h).wait_send()
        for by, flip in others:
            last_copy(p, by, flip).wait_send()
        if p:
            for by in (1, 2, 3):
                mid_copy(p, by).wait_send()
    store.wait()


def on_device(
    grid_latent, mesh_latent, g2m_send, g2m_src, g2m_dst, g2m_weight, halo_send, m2m_src, m2m_dst, m2m_weight,
    enc_msg_in, enc_msg_out, enc_upd_in, enc_upd_out, enc_gain,
    proc_msg_in, proc_msg_out, proc_upd_in, proc_upd_out, proc_gain,
):
    rows = g2m_weight.shape[1]
    width = grid_latent.shape[1]
    grid_blocks = grid_latent.shape[0] // rows
    blocks = mesh_latent.shape[0] // rows
    steps = proc_msg_in.shape[0]
    rim = halo_send.shape[1]
    peers = g2m_send.shape[1]
    hbm = pl.BlockSpec(memory_space=pl.ANY)

    sub = rows // PARTS
    flying = (4, grid_blocks, sub, width)
    staged = (3, 4, 4, 2, sub, width)
    holding = (4, 4, 4, 2, sub, width)
    dma = pltpu.SemaphoreType.DMA
    vm = pltpu.VMEM
    out = pl.pallas_call(
        whole_kernel,
        out_shape=jax.ShapeDtypeStruct((blocks, rows, width), BF16),
        in_specs=[hbm] * 20,
        out_specs=hbm,
        scratch_shapes=[
            vm((grid_blocks, rows, width), BF16),
            *[vm(w.shape, BF16) for w in (
                enc_msg_in, enc_msg_out, enc_upd_in, enc_upd_out,
                proc_msg_in, proc_msg_out, proc_upd_in, proc_upd_out)],
            vm((1, width), F32),
            vm((steps, width), F32),
            vm((blocks, rows, width), BF16),
            *[vm(v.shape, jnp.int32) for v in (g2m_src, g2m_dst, m2m_src, m2m_dst, halo_send)],
            vm((8, 256), jnp.int32),
            pltpu.SMEM((8, 256), jnp.int32),
            vm((rows, rows, g2m_dst.shape[1]), BF16),
            vm((steps, rows, rows, m2m_dst.shape[1]), BF16),
            vm(g2m_weight.shape, BF16),
            vm((blocks, rows, rows * (g2m_dst.shape[1] // blocks)), BF16),
            vm((steps, blocks, rows, rows * (m2m_dst.shape[1] // blocks)), BF16),
            vm((5, 4, 2, 4, rows, width), BF16),
            *[vm(flying, BF16)] * 4,
            *[vm(staged, BF16)] * 3,
            *[vm(holding, BF16)] * 4,
            vm((blocks, rows, width), BF16),
            vm((blocks, rows, width), BF16),
            vm((blocks + 2 * rim, rows, width), BF16),
            vm((blocks + 2 * rim, rows, width), BF16),
            vm((rim, rows, width), BF16),
            vm((rim, rows, width), BF16),
            vm((1, peers), jnp.int32),
            vm((3, 4, 1, peers), jnp.int32),
            pltpu.SMEM((3, 4, 1, peers), jnp.int32),
            dma((8,)), dma((19,)), dma((3, 3)), dma((3, 3)),
            dma((4, 2, 2)), dma((4, 2, 2)), dma((4, 2)), dma((4, 2)),
            dma((4, 3)), dma((4, 3)), dma((4, 4, 2)), dma((4, 4, 2)), dma((8,)),
            dma((steps, 2, 2)), dma((steps, 2, 2)),
        ],
        compiler_params=pltpu.CompilerParams(
            collective_id=0, has_side_effects=True, vmem_limit_bytes=62 * 2**20
        ),
        name="encoder_and_steps",
    )(
        g2m_src, g2m_dst, m2m_src, m2m_dst, halo_send,
        g2m_send, grid_latent.reshape(grid_blocks, rows, width), mesh_latent.reshape(blocks, rows, width),
        jnp.transpose(g2m_weight, (1, 2, 0)), jnp.transpose(m2m_weight, (0, 2, 3, 1)),
        enc_msg_in, enc_msg_out, enc_upd_in, enc_upd_out, enc_gain.reshape(1, width),
        proc_msg_in, proc_msg_out, proc_upd_in, proc_upd_out, proc_gain,
    )
    return out.reshape(blocks * rows, width)


def solution(mesh):
    both = P(("tile", "dom"), None)
    whole = P()
    placed = (
        both, both, both, both, both, P(("tile", "dom"), None, None), both, both, both,
        P(None, ("tile", "dom"), None, None),
    ) + (whole,) * 10
    return jax.shard_map(
        on_device, mesh=mesh, in_specs=placed, out_specs=both, check_vma=False
    )
```

```python
import functools

import jax
import jax.numpy as jnp
from jax import lax
from jax.experimental import pallas as pl
from jax.experimental.pallas import tpu as pltpu
from jax.sharding import PartitionSpec as P

MESH = pl.DeviceIdType.MESH
F32 = jnp.float32
BF16 = jnp.bfloat16


def silu(v):
    half = 0.5 * v
    return half + half * jnp.tanh(half)


def mm(a, b):
    return jnp.dot(a, b, preferred_element_type=F32)


def iota(shape, dim):
    return lax.broadcasted_iota(jnp.int32, shape, dim)


def total(mask, values, axis):
    return jnp.sum(jnp.where(mask, values, 0), axis=axis, keepdims=True)


def column(row):
    n = row.shape[1]
    return total(iota((n, n), 0) == iota((n, n), 1), row, 1)


def ranks(row):
    n = row.shape[1]
    key = row * n + iota((1, n), 1)
    return total(key < column(key), 1, 1)


def sort_by(rank, col):
    n = col.shape[0]
    return total(rank == iota((n, n), 1), col, 0)


def placed(place, row):
    n = place.shape[0]
    return total(iota((n, row.shape[1]), 0) == row, place, 0)


def loop(first, last, step):
    def body(i, _):
        step(i)
        return 0

    lax.fori_loop(first, last, body, 0)


PARTS = 4
LINES = (("x", "y", "z"), ("y", "z", "x"), ("z", "x", "y"), ("x", "y", "z"))
AXES = ("x", "y", "z")


def whole_kernel(
    g_src_h, g_dst_h, m_src_h, m_dst_h, halo_h,
    send_row, grid_latent, latent_in, g_weight, m_weight,
    a_in_h, a_out_h, e_in_h, e_out_h, e_gain_h, m_in_h, m_out_h, u_in_h, u_out_h, u_gain_h,
    out_h,
    a_in, a_out, e_in, e_out, m_in, m_out, u_in, u_out, e_gain, u_gain, latent,
    g_from, g_to, m_from, m_to, halo_of, index_v, index_s,
    lanes_g, lanes_m, raw, wt_g, wt_m, table,
    a00, a01, a02, a03, a10, a11, a12, a13, a20, a21, a22, a23, a30, a31, a32, a33,
    s0, s1, s2, s3, r0, r1, r2, r3,
    state, mine, ptable0, ptable1, payload0, payload1, own_row, rows_v, rows_s,
    chunk_sem, load_sem, row_s, row_r, ag_s, ag_r, relay_s, relay_r, mid_s, mid_r, last_s, last_r, keep_sem, local_sem,
    send_sem, recv_sem,
):
    blocks, rows, width = latent.shape
    grid_blocks = grid_latent.shape[0]
    sub = rows // PARTS
    rim = halo_of.shape[1]
    steps = m_in.shape[0]
    ptable, payload = (ptable0, ptable1), (payload0, payload1)
    ag = ((a00, a01, a02, a03), (a10, a11, a12, a13), (a20, a21, a22, a23), (a30, a31, a32, a33))
    stage, held = (s0, s1, s2, s3), (r0, r1, r2, r3)
    tile = lax.axis_index("tile")
    core = lax.rem(tile, 2)
    at = {"x": lax.axis_index("dom"), "y": lax.rem(tile // 2, 4), "z": tile // 8}

    def device(c, core_at):
        return (c["z"] * 4 + c["y"]) * 2 + core_at, c["x"]

    def moved(axis, by, flip=0):
        c = dict(at)
        c[axis] = lax.rem(at[axis] + by + 4, 4)
        return device(c, lax.rem(core + flip, 2))

    chunk = 4
    chunks = grid_blocks // chunk

    def chunk_load(h, i):
        n = h * (chunks // 2) + i
        return pltpu.make_async_copy(
            grid_latent.at[pl.ds(n * chunk, chunk)], (state, mine)[h].at[pl.ds(i * chunk, chunk)], chunk_sem.at[n])

    loads = [
        pltpu.make_async_copy(src, dst, load_sem.at[i])
        for i, (src, dst) in enumerate((
            (a_in_h, a_in), (a_out_h, a_out), (send_row, own_row),
            (g_src_h, g_from), (g_dst_h, g_to), (m_src_h, m_from), (m_dst_h, m_to), (halo_h, halo_of),
            (g_weight, lanes_g), (m_weight, lanes_m), (latent_in, latent), (e_gain_h, e_gain), (u_gain_h, u_gain),
            (e_in_h, e_in), (e_out_h, e_out), (m_in_h, m_in), (m_out_h, m_out), (u_in_h, u_in), (u_out_h, u_out),
        ))
    ]
    loads[0].start()
    chunk_load(0, 0).start()
    loads[1].start()
    loads[2].start()
    for i in range(1, chunks):
        chunk_load(i // (chunks // 2), i % (chunks // 2)).start()

    barrier = pltpu.get_barrier_semaphore()
    greeted = [moved(axis, by, flip) for axis in AXES for by in (1, 2, 3) for flip in (0, 1)] + [moved("x", 0, 1)]
    for peer in greeted:
        pl.semaphore_signal(barrier, inc=1, device_id=peer, device_id_type=MESH)

    def mlp(h, k):
        chunk_load(h, k).wait()
        i = h * (chunks // 2) + k
        x = (state, mine)[h][pl.ds(k * chunk, chunk)].reshape(chunk * rows, width)
        hidden = silu(mm(x, a_in[...])).astype(BF16)
        msg = mm(hidden, a_out[...]).astype(BF16).reshape(chunk, rows, width)
        table[0, i // 2, lax.rem(i, 2)] = msg
        for p in range(PARTS):
            ag[p][0][pl.ds(i * chunk, chunk)] = msg[:, p * sub:(p + 1) * sub]

    half = grid_blocks // 2

    def gather_copy(p, way, h):
        here = pl.ds(h * half, half)
        return pltpu.make_async_remote_copy(
            ag[p][0].at[here], ag[p][3 - 2 * way].at[here], ag_s.at[p, way, h], ag_r.at[p, way, h],
            device_id=moved(LINES[p][0], 1 - 2 * way), device_id_type=MESH)

    def relay_copy(p, way):
        here = pl.ds(way * half, half)
        return pltpu.make_async_remote_copy(
            ag[p][3 - 2 * way].at[here], ag[p][2].at[here], relay_s.at[p, way], relay_r.at[p, way],
            device_id=moved(LINES[p][0], 1 - 2 * way), device_id_type=MESH)

    def row_copy(a, by):
        axis = AXES[a]
        return pltpu.make_async_remote_copy(
            own_row, rows_v.at[a, at[axis]], row_s.at[a, by - 1], row_r.at[a, by - 1],
            device_id=moved(axis, by), device_id_type=MESH)

    loads[0].wait()
    loads[1].wait()
    loop(0, chunks // 2, functools.partial(mlp, 0))
    pl.semaphore_wait(barrier, len(greeted))
    for p in range(3):
        for way in (0, 1):
            gather_copy(p, way, 0).start()
    loads[2].wait()
    for a in range(3):
        for by in (1, 2, 3):
            row_copy(a, by).start()
    own_rows = [pltpu.make_async_copy(own_row, rows_v.at[a, at[AXES[a]]], local_sem.at[a]) for a in range(3)]
    for c in own_rows:
        c.start()
    loop(0, chunks // 2, functools.partial(mlp, 1))
    for p in range(3):
        for way in (0, 1):
            gather_copy(p, way, 1).start()

    for c in loads[3:]:
        c.start()

    def relays(p):
        for way in (0, 1):
            gather_copy(p, way, way).wait_recv()
            relay_copy(p, way).start()

    def near(p):
        for way in (0, 1):
            gather_copy(p, way, 1 - way).wait_recv()

    def far(p):
        for way in (0, 1):
            relay_copy(p, way).wait_recv()

    def spread(p):
        for h in (0, 1):
            for way in (0, 1):
                gather_copy(p, way, h).start()

    def held_at(p, b, j):
        return (j, b) if p == 2 else (b, j)

    def mid_copy(p, by, j):
        first, second, _ = LINES[p]
        b, k = held_at(p, at[second], lax.rem(at[first] + j, 4))
        return pltpu.make_async_remote_copy(
            stage[p].at[by - 1, j], held[p].at[b, k], mid_s.at[p, by - 1, j], mid_r.at[p, by - 1, j],
            device_id=moved(second, by), device_id_type=MESH)

    def select(p, js):
        first, second, third = LINES[p]
        a = AXES.index(first)

        def of(by, j):
            c = dict(at)
            c[second] = lax.rem(at[second] + by, 4)
            row = lax.rem(at[first] + j, 4)
            for k in range(8):
                c[third] = k // 2
                t, x = device(c, k % 2)
                yield k // 2, k % 2, ag[p][j][rows_s[a, row, 0, t * 4 + x]]

        for j in js:
            def put(by, _):
                for c3, k, got in of(by, j):
                    stage[p][by - 1, j, c3, k] = got
                return 0

            lax.fori_loop(1, 4, put, 0)
            b, row = held_at(p, at[second], lax.rem(at[first] + j, 4))
            for c3, k, got in of(0, j):
                held[p][b, row, c3, k] = got

    def pass_on(p, js):
        for j in js:
            for by in (1, 3, 2):
                mid_copy(p, by, j).start()

    def arrived(p, js):
        for j in js:
            loop(1, 4, lambda by: mid_copy(p, by, j).wait_recv())

    def landing(p, b):
        here = pl.ds(p * sub, sub)
        if p == 1:
            return table.at[1 + b, :, core, at["x"], here]
        if p == 2:
            return table.at[pl.ds(1, 4), at["y"], core, b, here]
        return table.at[1 + at["z"], b, core, :, here]

    def leaving(p, b, c3, k):
        return held[p].at[:, b, c3, k] if p == 2 else held[p].at[b, :, c3, k]

    def last_copy(p, bi, k):
        _, second, axis = LINES[p]
        by, flip = k // 2, lax.rem(k, 2)
        b = lax.rem(at[second] + bi, 4)
        return pltpu.make_async_remote_copy(
            leaving(p, b, lax.rem(at[axis] + by, 4), lax.rem(core + flip, 2)), landing(p, b),
            last_s.at[p, bi, k], last_r.at[p, bi, k],
            device_id=moved(axis, by, flip), device_id_type=MESH)

    def keep_copy(p, bi):
        _, second, axis = LINES[p]
        b = lax.rem(at[second] + bi, 4)
        return pltpu.make_async_copy(leaving(p, b, at[axis], core), landing(p, b), keep_sem.at[p, bi])

    def deliver(p, first, last):
        def one(bi):
            loop(1, 8, lambda k: last_copy(p, bi, k).start())
            keep_copy(p, bi).start()

        loop(first, last, one)

    slots_g = g_to.shape[1] // blocks
    slots_m = m_to.shape[1] // blocks
    packed = 16

    def listed(r):
        return lambda k: index_s[r, k]

    g_order, g_src, m_order, m_src, perm, place, halo_at = [listed(r) for r in range(7)]

    def index_lists():
        halo_row = halo_of[...]
        named = iota((blocks, rim), 0) == halo_row
        first = jnp.min(
            jnp.where(named, iota((blocks, rim), 1), rim + iota((blocks, rim), 0)), axis=1, keepdims=True)
        first_row = total(iota((blocks, blocks), 0) == iota((blocks, blocks), 1), first, 0)
        spot = total(first_row < first, 1, 1)
        rank_g = ranks(placed(spot, g_to[...]))
        rank_m = ranks(placed(spot, m_to[...]))
        m_row = m_from[...]
        own = jnp.where(m_row < blocks, placed(spot, jnp.minimum(m_row, blocks - 1)), m_row)
        ng, nm = g_to.shape[1], m_to.shape[1]
        for r, row in enumerate((
            sort_by(rank_g, iota((ng, 1), 0)), sort_by(rank_g, column(g_from[...])),
            sort_by(rank_m, iota((nm, 1), 0)), sort_by(rank_m, column(own)),
            sort_by(spot, iota((blocks, 1), 0)),
            total(iota((blocks, blocks), 0) == iota((blocks, blocks), 1), spot, 0),
            placed(spot, halo_row),
        )):
            index_v[pl.ds(r, 1), pl.ds(0, row.shape[1])] = row
        copy = pltpu.make_async_copy(index_v, index_s, local_sem.at[7])
        copy.start()
        return copy

    def unpack(lanes, base, first, last):
        def body(q, _):
            x = lanes[pl.ds(q * packed, packed)]
            tiles = jnp.swapaxes(jnp.swapaxes(x, 1, 2), 0, 1)
            raw[pl.ds(base, tiles.shape[0]), pl.ds(q * packed, packed)] = tiles
            return 0
        lax.fori_loop(first, last, body, 0)

    def prepare(order, base, wt, slots):
        def body(b, _):
            cat = jnp.concatenate([raw[base + order(b * slots + k)] for k in range(slots)], axis=0)
            wt[b] = cat.T
            return 0
        lax.fori_loop(0, blocks, body, 0)

    groups = rows // packed
    for c in loads[3:8]:
        c.wait()
    lists = index_lists()
    loads[8].wait()
    unpack(lanes_g, 0, 0, 2)
    for p in range(3):
        relays(p)
    unpack(lanes_g, 0, 2, groups)
    for a in range(3):
        own_rows[a].wait()
        for by in (1, 2, 3):
            row_copy(a, by).wait()
    to_scalar = pltpu.make_async_copy(rows_v, rows_s, local_sem.at[0])
    to_scalar.start()
    to_scalar.wait()
    lists.wait()

    every, close = (0, 1, 3, 2), (0, 1, 3)
    select(0, (0,))
    select(1, (0,))
    near(0)
    spread(3)
    select(0, (1, 3))
    pass_on(0, close)
    near(1)
    select(1, (1, 3))
    pass_on(1, close)
    near(2)
    select(2, close)
    far(0)
    select(0, (2,))
    pass_on(0, (2,))
    far(1)
    select(1, (2,))
    pass_on(1, (2,))
    prepare(g_order, 0, wt_g, slots_g)
    far(2)
    select(2, (2,))
    relays(3)
    loads[9].wait()
    half_tiles = raw.shape[0] // steps
    unpack(lanes_m.at[0], 0, 0, 2)
    select(3, (0,))
    near(3)
    pass_on(2, every)
    select(3, (1, 3))
    deliver(0, 0, 1)
    far(3)
    select(3, (2,))
    pass_on(3, every)
    unpack(lanes_m.at[0], 0, 2, groups)
    arrived(0, every)
    deliver(0, 1, 4)
    unpack(lanes_m.at[1], half_tiles, 0, groups)
    for s in range(steps):
        prepare(m_order, s * half_tiles, wt_m.at[s], slots_m)
    arrived(1, every)
    arrived(2, close)
    deliver(1, 0, 4)
    deliver(3, 0, 1)
    arrived(2, (2,))
    deliver(2, 0, 4)
    arrived(3, every)
    deliver(3, 1, 4)
    for c in loads[10:]:
        c.wait()
    for p in range(PARTS):
        def landed(bi):
            loop(1, 8, lambda k: last_copy(p, bi, k).wait_recv())
            keep_copy(p, bi).wait()

        loop(0, 4, landed)

    n_dom = lax.axis_size("dom")
    upper, lower = moved("x", 1), moved("x", 3)
    quarter = blocks // 4
    half_rim = rim // 2

    def halo(s, h):
        src = payload[s].at[pl.ds(h * half_rim, half_rim)]
        up = pltpu.make_async_remote_copy(
            src, ptable[s].at[pl.ds(blocks + h * half_rim, half_rim)],
            send_sem.at[s, 0, h], recv_sem.at[s, 0, h], device_id=upper, device_id_type=MESH)
        down = pltpu.make_async_remote_copy(
            src, ptable[s].at[pl.ds(blocks + rim + h * half_rim, half_rim)],
            send_sem.at[s, 1, h], recv_sem.at[s, 1, h], device_id=lower, device_id_type=MESH)
        return up, down

    def from_grid(i):
        return table[i // 32, lax.rem(i // 8, 4), lax.rem(i // 4, 2), lax.rem(i, 4)]

    def summed(load, idx, wt, slots, c):
        parts = []
        for i in range(quarter):
            p = c * quarter + i
            got = jnp.concatenate([load(idx(p * slots + k)) for k in range(slots)], axis=0)
            parts.append(mm(wt[p], got).astype(BF16))
        return jnp.concatenate(parts, axis=0)

    def update(old, agg, w_in, w_out, gain):
        pre = mm(old, w_in[pl.ds(0, width), :]) + mm(agg, w_in[pl.ds(width, width), :])
        o = mm(silu(pre).astype(BF16), w_out[...])
        mean = jnp.mean(o, axis=1, keepdims=True)
        cen = o - mean
        var = jnp.mean(cen * cen, axis=1, keepdims=True)
        normed = cen * lax.rsqrt(var + 1e-05) * gain
        return (old.astype(F32) + normed).astype(BF16)

    def message(s, c, new):
        h = silu(mm(new, m_in[s])).astype(BF16)
        msg = mm(h, m_out[s]).astype(BF16)
        msg = msg.reshape(quarter, rows, width)
        mine[pl.ds(c * quarter, quarter)] = msg
        ptable[s][pl.ds(c * quarter, quarter)] = msg

    def push(s, h):
        for i in range(half_rim):
            payload[s][h * half_rim + i] = mine[halo_at(h * half_rim + i)]
        for c in halo(s, h):
            c.start()

    def enc_chunk(c):
        agg = summed(from_grid, g_src, wt_g, slots_g, c)
        old = jnp.concatenate([latent[perm(c * quarter + i)] for i in range(quarter)], axis=0)
        new = update(old, agg, e_in, e_out, e_gain[...])
        state[pl.ds(c * quarter, quarter)] = new.reshape(quarter, rows, width)
        message(0, c, new)

    def proc_chunk(s, c):
        agg = summed(lambda i: ptable[s][i], m_src, wt_m.at[s], slots_m, c)
        old = state[pl.ds(c * quarter, quarter)].reshape(quarter * rows, width)
        new = update(old, agg, u_in.at[s], u_out.at[s], u_gain[pl.ds(s, 1), :])
        state[pl.ds(c * quarter, quarter)] = new.reshape(quarter, rows, width)
        if s + 1 < steps:
            message(s + 1, c, new)

    def rest(chunk, first):
        def body(c, _):
            chunk(c)
            return 0
        lax.fori_loop(first, 4, body, 0)

    enc_chunk(0)
    push(0, 0)
    enc_chunk(1)
    push(0, 1)
    rest(enc_chunk, 2)
    for s in range(steps):
        for h in range(2):
            for c in halo(s, h):
                c.wait()
        if s + 1 < steps:
            proc_chunk(s, 0)
            push(s + 1, 0)
            proc_chunk(s, 1)
            push(s + 1, 1)
            rest(functools.partial(proc_chunk, s), 2)
        else:
            rest(functools.partial(proc_chunk, s), 0)

    def restore(b, _):
        mine[b] = state[place(b)]
        return 0

    lax.fori_loop(0, blocks, restore, 0)
    store = pltpu.make_async_copy(mine, out_h, local_sem.at[0])
    store.start()
    for p in range(PARTS):
        for way in (0, 1):
            relay_copy(p, way).wait_send()
            for h in (0, 1):
                gather_copy(p, way, h).wait_send()
        def sent(j):
            loop(1, 4, lambda by: mid_copy(p, by, j).wait_send())
            loop(1, 8, lambda k: last_copy(p, j, k).wait_send())

        loop(0, 4, sent)
    store.wait()


def on_device(
    grid_latent, mesh_latent, g2m_send, g2m_src, g2m_dst, g2m_weight, halo_send, m2m_src, m2m_dst, m2m_weight,
    enc_msg_in, enc_msg_out, enc_upd_in, enc_upd_out, enc_gain,
    proc_msg_in, proc_msg_out, proc_upd_in, proc_upd_out, proc_gain,
):
    rows = g2m_weight.shape[1]
    width = grid_latent.shape[1]
    grid_blocks = grid_latent.shape[0] // rows
    blocks = mesh_latent.shape[0] // rows
    steps = proc_msg_in.shape[0]
    rim = halo_send.shape[1]
    peers = g2m_send.shape[1]
    hbm = pl.BlockSpec(memory_space=pl.ANY)

    sub = rows // PARTS
    flying = (grid_blocks, sub, width)
    staged = (3, 4, 4, 2, sub, width)
    holding = (4, 4, 4, 2, sub, width)
    dma = pltpu.SemaphoreType.DMA
    vm = pltpu.VMEM
    out = pl.pallas_call(
        whole_kernel,
        out_shape=jax.ShapeDtypeStruct((blocks, rows, width), BF16),
        in_specs=[hbm] * 20,
        out_specs=hbm,
        scratch_shapes=[
            *[vm(w.shape, BF16) for w in (
                enc_msg_in, enc_msg_out, enc_upd_in, enc_upd_out,
                proc_msg_in, proc_msg_out, proc_upd_in, proc_upd_out)],
            vm((1, width), F32),
            vm((steps, width), F32),
            vm((blocks, rows, width), BF16),
            *[vm(v.shape, jnp.int32) for v in (g2m_src, g2m_dst, m2m_src, m2m_dst, halo_send)],
            vm((8, 256), jnp.int32),
            pltpu.SMEM((8, 256), jnp.int32),
            vm((rows, rows, g2m_dst.shape[1]), BF16),
            vm((steps, rows, rows, m2m_dst.shape[1]), BF16),
            vm(g2m_weight.shape, BF16),
            vm((blocks, rows, rows * (g2m_dst.shape[1] // blocks)), BF16),
            vm((steps, blocks, rows, rows * (m2m_dst.shape[1] // blocks)), BF16),
            vm((5, 4, 2, 4, rows, width), BF16),
            *[vm(flying, BF16)] * 16,
            *[vm(staged, BF16)] * 4,
            *[vm(holding, BF16)] * 4,
            vm((blocks, rows, width), BF16),
            vm((blocks, rows, width), BF16),
            vm((blocks + 2 * rim, rows, width), BF16),
            vm((blocks + 2 * rim, rows, width), BF16),
            vm((rim, rows, width), BF16),
            vm((rim, rows, width), BF16),
            vm((1, peers), jnp.int32),
            vm((3, 4, 1, peers), jnp.int32),
            pltpu.SMEM((3, 4, 1, peers), jnp.int32),
            dma((8,)), dma((19,)), dma((3, 3)), dma((3, 3)),
            dma((4, 2, 2)), dma((4, 2, 2)), dma((4, 2)), dma((4, 2)),
            dma((4, 3, 4)), dma((4, 3, 4)), dma((4, 4, 8)), dma((4, 4, 8)), dma((4, 4)), dma((8,)),
            dma((steps, 2, 2)), dma((steps, 2, 2)),
        ],
        compiler_params=pltpu.CompilerParams(
            collective_id=0, has_side_effects=True, vmem_limit_bytes=62 * 2**20
        ),
        name="encoder_and_steps",
    )(
        g2m_src, g2m_dst, m2m_src, m2m_dst, halo_send,
        g2m_send, grid_latent.reshape(grid_blocks, rows, width), mesh_latent.reshape(blocks, rows, width),
        jnp.transpose(g2m_weight, (1, 2, 0)), jnp.transpose(m2m_weight, (0, 2, 3, 1)),
        enc_msg_in, enc_msg_out, enc_upd_in, enc_upd_out, enc_gain.reshape(1, width),
        proc_msg_in, proc_msg_out, proc_upd_in, proc_upd_out, proc_gain,
    )
    return out.reshape(blocks * rows, width)


def solution(mesh):
    both = P(("tile", "dom"), None)
    whole = P()
    placed = (
        both, both, both, both, both, P(("tile", "dom"), None, None), both, both, both,
        P(None, ("tile", "dom"), None, None),
    ) + (whole,) * 10
    return jax.shard_map(
        on_device, mesh=mesh, in_specs=placed, out_specs=both, check_vma=False
    )
```

```python
import functools

import jax
import jax.numpy as jnp
from jax import lax
from jax.experimental import pallas as pl
from jax.experimental.pallas import tpu as pltpu
from jax.sharding import PartitionSpec as P

MESH = pl.DeviceIdType.MESH
F32 = jnp.float32
BF16 = jnp.bfloat16


def silu(v):
    half = 0.5 * v
    return half + half * jnp.tanh(half)


def mm(a, b):
    return jnp.dot(a, b, preferred_element_type=F32)


def iota(shape, dim):
    return lax.broadcasted_iota(jnp.int32, shape, dim)


def total(mask, values, axis):
    return jnp.sum(jnp.where(mask, values, 0), axis=axis, keepdims=True)


def column(row):
    n = row.shape[1]
    return total(iota((n, n), 0) == iota((n, n), 1), row, 1)


def ranks(row):
    n = row.shape[1]
    key = row * n + iota((1, n), 1)
    return total(key < column(key), 1, 1)


def sort_by(rank, col):
    n = col.shape[0]
    return total(rank == iota((n, n), 1), col, 0)


def placed(place, row):
    n = place.shape[0]
    return total(iota((n, row.shape[1]), 0) == row, place, 0)


def loop(first, last, step):
    def body(i, _):
        step(i)
        return 0

    lax.fori_loop(first, last, body, 0)


PARTS = 4
LINES = (("x", "y", "z"), ("y", "z", "x"), ("z", "x", "y"), ("x", "y", "z"))
AXES = ("x", "y", "z")


def whole_kernel(
    g_src_h, g_dst_h, m_src_h, m_dst_h, halo_h,
    send_row, grid_latent, latent_in, g_weight, m_weight,
    a_in_h, a_out_h, e_in_h, e_out_h, e_gain_h, m_in_h, m_out_h, u_in_h, u_out_h, u_gain_h,
    out_h,
    a_in, a_out, e_in, e_out, m_in, m_out, u_in, u_out, e_gain, u_gain, latent,
    g_from, g_to, m_from, m_to, halo_of, index_v, index_s,
    lanes_g, lanes_m, raw, wt_g, wt_m, table,
    a00, a01, a02, a03, a10, a11, a12, a13, a20, a21, a22, a23, a30, a31, a32, a33,
    s0, s1, s2, s3, r0, r1, r2, r3,
    state, mine, ptable0, ptable1, payload0, payload1, own_row, rows_v, rows_s,
    chunk_sem, load_sem, row_s, row_r, ag_s, ag_r, relay_s, relay_r, mid_s, mid_r, last_s, last_r, keep_sem, local_sem,
    send_sem, recv_sem,
):
    blocks, rows, width = latent.shape
    grid_blocks = grid_latent.shape[0]
    sub = rows // PARTS
    rim = halo_of.shape[1]
    steps = m_in.shape[0]
    ptable, payload = (ptable0, ptable1), (payload0, payload1)
    ag = ((a00, a01, a02, a03), (a10, a11, a12, a13), (a20, a21, a22, a23), (a30, a31, a32, a33))
    stage, held = (s0, s1, s2, s3), (r0, r1, r2, r3)
    tile = lax.axis_index("tile")
    core = lax.rem(tile, 2)
    at = {"x": lax.axis_index("dom"), "y": lax.rem(tile // 2, 4), "z": tile // 8}

    def device(c, core_at):
        return (c["z"] * 4 + c["y"]) * 2 + core_at, c["x"]

    def moved(axis, by, flip=0):
        c = dict(at)
        c[axis] = lax.rem(at[axis] + by + 4, 4)
        return device(c, lax.rem(core + flip, 2))

    chunk = 4
    chunks = grid_blocks // chunk

    def chunk_load(h, i):
        n = h * (chunks // 2) + i
        return pltpu.make_async_copy(
            grid_latent.at[pl.ds(n * chunk, chunk)], (state, mine)[h].at[pl.ds(i * chunk, chunk)], chunk_sem.at[n])

    loads = [
        pltpu.make_async_copy(src, dst, load_sem.at[i])
        for i, (src, dst) in enumerate((
            (a_in_h, a_in), (a_out_h, a_out), (send_row, own_row),
            (g_src_h, g_from), (g_dst_h, g_to), (m_src_h, m_from), (m_dst_h, m_to), (halo_h, halo_of),
            (g_weight, lanes_g), (m_weight, lanes_m), (latent_in, latent), (e_gain_h, e_gain), (u_gain_h, u_gain),
            (e_in_h, e_in), (e_out_h, e_out), (m_in_h, m_in), (m_out_h, m_out), (u_in_h, u_in), (u_out_h, u_out),
        ))
    ]
    loads[0].start()
    chunk_load(0, 0).start()
    loads[1].start()
    loads[2].start()
    for i in range(1, chunks):
        chunk_load(i // (chunks // 2), i % (chunks // 2)).start()

    barrier = pltpu.get_barrier_semaphore()
    greeted = [moved(axis, by, flip) for axis in AXES for by in (1, 2, 3) for flip in (0, 1)] + [moved("x", 0, 1)]
    for peer in greeted:
        pl.semaphore_signal(barrier, inc=1, device_id=peer, device_id_type=MESH)

    def mlp(h, k):
        chunk_load(h, k).wait()
        i = h * (chunks // 2) + k
        x = (state, mine)[h][pl.ds(k * chunk, chunk)].reshape(chunk * rows, width)
        hidden = silu(mm(x, a_in[...])).astype(BF16)
        msg = mm(hidden, a_out[...]).astype(BF16).reshape(chunk, rows, width)
        table[0, i // 2, lax.rem(i, 2)] = msg
        for p in range(PARTS):
            ag[p][0][pl.ds(i * chunk, chunk)] = msg[:, p * sub:(p + 1) * sub]

    half = grid_blocks // 2

    def gather_copy(p, way, h):
        here = pl.ds(h * half, half)
        return pltpu.make_async_remote_copy(
            ag[p][0].at[here], ag[p][3 - 2 * way].at[here], ag_s.at[p, way, h], ag_r.at[p, way, h],
            device_id=moved(LINES[p][0], 1 - 2 * way), device_id_type=MESH)

    def relay_copy(p, way):
        here = pl.ds(way * half, half)
        return pltpu.make_async_remote_copy(
            ag[p][3 - 2 * way].at[here], ag[p][2].at[here], relay_s.at[p, way], relay_r.at[p, way],
            device_id=moved(LINES[p][0], 1 - 2 * way), device_id_type=MESH)

    def row_copy(a, by):
        axis = AXES[a]
        return pltpu.make_async_remote_copy(
            own_row, rows_v.at[a, at[axis]], row_s.at[a, by - 1], row_r.at[a, by - 1],
            device_id=moved(axis, by), device_id_type=MESH)

    loads[0].wait()
    loads[1].wait()
    loop(0, chunks // 2, functools.partial(mlp, 0))
    pl.semaphore_wait(barrier, len(greeted))
    for p in range(3):
        for way in (0, 1):
            gather_copy(p, way, 0).start()
    loads[2].wait()
    for a in range(3):
        for by in (1, 2, 3):
            row_copy(a, by).start()
    own_rows = [pltpu.make_async_copy(own_row, rows_v.at[a, at[AXES[a]]], local_sem.at[a]) for a in range(3)]
    for c in own_rows:
        c.start()
    loop(0, chunks // 2, functools.partial(mlp, 1))
    for p in range(3):
        for way in (0, 1):
            gather_copy(p, way, 1).start()

    for c in loads[3:]:
        c.start()

    def relays(p):
        for way in (0, 1):
            gather_copy(p, way, way).wait_recv()
            relay_copy(p, way).start()

    def near(p):
        for way in (0, 1):
            gather_copy(p, way, 1 - way).wait_recv()

    def far(p):
        for way in (0, 1):
            relay_copy(p, way).wait_recv()

    def spread(p):
        for h in (0, 1):
            for way in (0, 1):
                gather_copy(p, way, h).start()

    def spread_out(p):
        for way in (0, 1):
            relay_copy(p, way).wait_send()
            for h in (0, 1):
                gather_copy(p, way, h).wait_send()

    def held_at(p, b, j):
        return (j, b) if p == 2 else (b, j)

    def mid_copy(p, by, j):
        first, second, _ = LINES[p]
        b, k = held_at(p, at[second], lax.rem(at[first] + j, 4))
        return pltpu.make_async_remote_copy(
            stage[p].at[by - 1, j], held[p].at[b, k], mid_s.at[p, by - 1, j], mid_r.at[p, by - 1, j],
            device_id=moved(second, by), device_id_type=MESH)

    def select(p, js):
        first, second, third = LINES[p]
        a = AXES.index(first)

        def of(by, j):
            c = dict(at)
            c[second] = lax.rem(at[second] + by, 4)
            row = lax.rem(at[first] + j, 4)
            for k in range(8):
                c[third] = k // 2
                t, x = device(c, k % 2)
                yield k // 2, k % 2, ag[p][j][rows_s[a, row, 0, t * 4 + x]]

        for j in js:
            def put(by, _):
                for c3, k, got in of(by, j):
                    stage[p][by - 1, j, c3, k] = got
                return 0

            lax.fori_loop(1, 4, put, 0)
            b, row = held_at(p, at[second], lax.rem(at[first] + j, 4))
            for c3, k, got in of(0, j):
                held[p][b, row, c3, k] = got

    def pass_on(p, js):
        for j in js:
            for by in (1, 3, 2):
                mid_copy(p, by, j).start()

    def arrived(p, js):
        for j in js:
            loop(1, 4, lambda by: mid_copy(p, by, j).wait_recv())

    def landing(p, b):
        here = pl.ds(p * sub, sub)
        if p == 1:
            return table.at[1 + b, :, core, at["x"], here]
        if p == 2:
            return table.at[pl.ds(1, 4), at["y"], core, b, here]
        return table.at[1 + at["z"], b, core, :, here]

    def leaving(p, b, c3, k):
        return held[p].at[:, b, c3, k] if p == 2 else held[p].at[b, :, c3, k]

    def last_copy(p, bi, k):
        _, second, axis = LINES[p]
        by, flip = k // 2, lax.rem(k, 2)
        b = lax.rem(at[second] + bi, 4)
        return pltpu.make_async_remote_copy(
            leaving(p, b, lax.rem(at[axis] + by, 4), lax.rem(core + flip, 2)), landing(p, b),
            last_s.at[p, bi, k], last_r.at[p, bi, k],
            device_id=moved(axis, by, flip), device_id_type=MESH)

    def keep_copy(p, bi):
        _, second, axis = LINES[p]
        b = lax.rem(at[second] + bi, 4)
        return pltpu.make_async_copy(leaving(p, b, at[axis], core), landing(p, b), keep_sem.at[p, bi])

    def deliver(p, first, last):
        def one(bi):
            loop(1, 8, lambda k: last_copy(p, bi, k).start())
            keep_copy(p, bi).start()

        loop(first, last, one)

    slots_g = g_to.shape[1] // blocks
    slots_m = m_to.shape[1] // blocks
    packed = 16

    def listed(r):
        return lambda k: index_s[r, k]

    g_order, g_src, m_order, m_src, perm, place, halo_at = [listed(r) for r in range(7)]

    def index_lists():
        halo_row = halo_of[...]
        named = iota((blocks, rim), 0) == halo_row
        first = jnp.min(
            jnp.where(named, iota((blocks, rim), 1), rim + iota((blocks, rim), 0)), axis=1, keepdims=True)
        first_row = total(iota((blocks, blocks), 0) == iota((blocks, blocks), 1), first, 0)
        spot = total(first_row < first, 1, 1)
        rank_g = ranks(placed(spot, g_to[...]))
        rank_m = ranks(placed(spot, m_to[...]))
        m_row = m_from[...]
        own = jnp.where(m_row < blocks, placed(spot, jnp.minimum(m_row, blocks - 1)), m_row)
        ng, nm = g_to.shape[1], m_to.shape[1]
        for r, row in enumerate((
            sort_by(rank_g, iota((ng, 1), 0)), sort_by(rank_g, column(g_from[...])),
            sort_by(rank_m, iota((nm, 1), 0)), sort_by(rank_m, column(own)),
            sort_by(spot, iota((blocks, 1), 0)),
            total(iota((blocks, blocks), 0) == iota((blocks, blocks), 1), spot, 0),
            placed(spot, halo_row),
        )):
            index_v[pl.ds(r, 1), pl.ds(0, row.shape[1])] = row
        copy = pltpu.make_async_copy(index_v, index_s, local_sem.at[7])
        copy.start()
        return copy

    def unpack(lanes, base, first, last):
        def body(q, _):
            x = lanes[pl.ds(q * packed, packed)]
            tiles = jnp.swapaxes(jnp.swapaxes(x, 1, 2), 0, 1)
            raw[pl.ds(base, tiles.shape[0]), pl.ds(q * packed, packed)] = tiles
            return 0
        lax.fori_loop(first, last, body, 0)

    def prepare(order, base, wt, slots):
        def body(b, _):
            cat = jnp.concatenate([raw[base + order(b * slots + k)] for k in range(slots)], axis=0)
            wt[b] = cat.T
            return 0
        lax.fori_loop(0, blocks, body, 0)

    def rim_weights(s, base, h):
        side = iota((rows, 2 * rows), 1) // rows
        wide = 2 * rows

        def one(n):
            b = h * (blocks // 2) + n
            src = [m_src(b * slots_m + k) for k in range(slots_m)]
            tiles = [raw[base + m_order(b * slots_m + k)] for k in range(slots_m)]
            own = [jnp.where(src[k] < blocks, tiles[k], jnp.zeros_like(tiles[k])) for k in range(slots_m)]
            wt_m[s, b] = jnp.concatenate(own, axis=0).T
            twice = jnp.concatenate([t for t in tiles for _ in (0, 1)], axis=0).T.astype(F32)
            for pair in range(rim):
                acc = jnp.zeros((rows, wide), F32)
                for k in range(slots_m):
                    hit = side + (blocks + 2 * pair) == src[k]
                    acc = acc + jnp.where(hit, twice[:, k * wide:(k + 1) * wide], 0.0)
                q, lane = pair // (rim // 2), pair % (rim // 2)
                ag[s][2 * q + h][pl.ds(n * PARTS, PARTS), :, pl.ds(lane * wide, wide)] = (
                    acc.astype(BF16).reshape(PARTS, sub, wide))

        loop(0, blocks // 2, one)

    groups = rows // packed
    for c in loads[3:8]:
        c.wait()
    lists = index_lists()
    loads[8].wait()
    unpack(lanes_g, 0, 0, 2)
    for p in range(3):
        relays(p)
    unpack(lanes_g, 0, 2, groups)
    for a in range(3):
        own_rows[a].wait()
        for by in (1, 2, 3):
            row_copy(a, by).wait()
    to_scalar = pltpu.make_async_copy(rows_v, rows_s, local_sem.at[0])
    to_scalar.start()
    to_scalar.wait()
    lists.wait()

    every, close = (0, 1, 3, 2), (0, 1, 3)
    select(0, (0,))
    select(1, (0,))
    near(0)
    spread(3)
    select(0, (1, 3))
    pass_on(0, close)
    near(1)
    select(1, (1, 3))
    pass_on(1, close)
    near(2)
    select(2, close)
    far(0)
    select(0, (2,))
    pass_on(0, (2,))
    far(1)
    select(1, (2,))
    pass_on(1, (2,))
    prepare(g_order, 0, wt_g, slots_g)
    far(2)
    select(2, (2,))
    relays(3)
    loads[9].wait()
    half_tiles = raw.shape[0] // steps
    unpack(lanes_m.at[0], 0, 0, groups)
    select(3, (0,))
    near(3)
    pass_on(2, every)
    select(3, (1, 3))
    deliver(0, 0, 1)
    unpack(lanes_m.at[1], half_tiles, 0, groups)
    far(3)
    select(3, (2,))
    pass_on(3, every)
    for p in range(2):
        spread_out(p)
    rim_weights(0, 0, 0)
    arrived(0, every)
    deliver(0, 1, 4)
    rim_weights(0, 0, 1)
    rim_weights(1, half_tiles, 0)
    arrived(1, every)
    arrived(2, close)
    deliver(1, 0, 4)
    deliver(3, 0, 1)
    rim_weights(1, half_tiles, 1)
    arrived(2, (2,))
    deliver(2, 0, 4)
    arrived(3, every)
    deliver(3, 1, 4)
    for c in loads[10:]:
        c.wait()
    for p in range(PARTS):
        def landed(bi):
            loop(1, 8, lambda k: last_copy(p, bi, k).wait_recv())
            keep_copy(p, bi).wait()

        loop(0, 4, landed)

    n_dom = lax.axis_size("dom")
    upper, lower = moved("x", 1), moved("x", 3)
    quarter = blocks // 4
    half_rim = rim // 2

    def halo(s, h):
        src = payload[s].at[pl.ds(h * half_rim, half_rim)]
        up = pltpu.make_async_remote_copy(
            src, ptable[s].at[pl.ds(h * half_rim, half_rim)],
            send_sem.at[s, 0, h], recv_sem.at[s, 0, h], device_id=upper, device_id_type=MESH)
        down = pltpu.make_async_remote_copy(
            src, ptable[s].at[pl.ds(rim + h * half_rim, half_rim)],
            send_sem.at[s, 1, h], recv_sem.at[s, 1, h], device_id=lower, device_id_type=MESH)
        return up, down

    def from_grid(i):
        return table[i // 32, lax.rem(i // 8, 4), lax.rem(i // 4, 2), lax.rem(i, 4)]

    def tiles_sum(load, idx, wt, slots, p):
        got = jnp.concatenate([load(idx(p * slots + k)) for k in range(slots)], axis=0)
        return mm(wt[p], got)

    def own_part(s):
        def one(p):
            acc = tiles_sum(lambda i: mine[jnp.minimum(i, blocks - 1)], m_src, wt_m.at[s], slots_m, p)
            high = acc.astype(BF16)
            at_p = p // 8, lax.rem(p // 4, 2), lax.rem(p, 4)
            table[(0, *at_p)] = high
            table[(1, *at_p)] = (acc - high.astype(F32)).astype(BF16)

        loop(0, blocks, one)

    def rim_part(s, h, k):
        c = 2 * h + k
        some = pl.ds(k * quarter * PARTS, quarter * PARTS)
        acc = jnp.zeros((quarter * rows, width), F32)
        for q in (0, 1):
            dense = ag[s][2 * q + h][some].reshape(quarter * rows, rim * rows)
            acc = acc + mm(dense, ptable[s][pl.ds(q * rim, rim)].reshape(rim * rows, width))
        at_c = c // 2, lax.rem(c, 2)
        for level in (0, 1):
            acc = acc + table[(level, *at_c)].reshape(quarter * rows, width).astype(F32)
        return acc.astype(BF16)

    def update(old, agg, w_in, w_out, gain):
        pre = mm(old, w_in[pl.ds(0, width), :]) + mm(agg, w_in[pl.ds(width, width), :])
        o = mm(silu(pre).astype(BF16), w_out[...])
        mean = jnp.mean(o, axis=1, keepdims=True)
        cen = o - mean
        var = jnp.mean(cen * cen, axis=1, keepdims=True)
        normed = cen * lax.rsqrt(var + 1e-05) * gain
        return (old.astype(F32) + normed).astype(BF16)

    def message(s, c, new):
        h = silu(mm(new, m_in[s])).astype(BF16)
        msg = mm(h, m_out[s]).astype(BF16)
        mine[pl.ds(c * quarter, quarter)] = msg.reshape(quarter, rows, width)

    def push(s, h):
        for i in range(half_rim):
            payload[s][h * half_rim + i] = mine[halo_at(h * half_rim + i)]
        for c in halo(s, h):
            c.start()

    def enc_chunk(c):
        agg = jnp.concatenate([
            tiles_sum(from_grid, g_src, wt_g, slots_g, c * quarter + i).astype(BF16) for i in range(quarter)], axis=0)
        old = jnp.concatenate([latent[perm(c * quarter + i)] for i in range(quarter)], axis=0)
        new = update(old, agg, e_in, e_out, e_gain[...])
        state[pl.ds(c * quarter, quarter)] = new.reshape(quarter, rows, width)
        message(0, c, new)

    def proc_chunk(s, h, k):
        c = 2 * h + k
        old = state[pl.ds(c * quarter, quarter)].reshape(quarter * rows, width)
        new = update(old, rim_part(s, h, k), u_in.at[s], u_out.at[s], u_gain[pl.ds(s, 1), :])
        state[pl.ds(c * quarter, quarter)] = new.reshape(quarter, rows, width)
        if s + 1 < steps:
            message(s + 1, c, new)

    enc_chunk(0)
    push(0, 0)
    enc_chunk(1)
    push(0, 1)
    loop(2, 4, enc_chunk)
    for s in range(steps):
        own_part(s)
        for h in range(2):
            for c in halo(s, h):
                c.wait()
        if s + 1 < steps:
            proc_chunk(s, 0, 0)
            push(s + 1, 0)
            proc_chunk(s, 0, 1)
            push(s + 1, 1)
        else:
            loop(0, 2, functools.partial(proc_chunk, s, 0))
        loop(0, 2, functools.partial(proc_chunk, s, 1))

    def restore(b, _):
        mine[b] = state[place(b)]
        return 0

    lax.fori_loop(0, blocks, restore, 0)
    store = pltpu.make_async_copy(mine, out_h, local_sem.at[0])
    store.start()
    for p in range(PARTS):
        if p >= 2:
            spread_out(p)

        def sent(j):
            loop(1, 4, lambda by: mid_copy(p, by, j).wait_send())
            loop(1, 8, lambda k: last_copy(p, j, k).wait_send())

        loop(0, 4, sent)
    store.wait()


def on_device(
    grid_latent, mesh_latent, g2m_send, g2m_src, g2m_dst, g2m_weight, halo_send, m2m_src, m2m_dst, m2m_weight,
    enc_msg_in, enc_msg_out, enc_upd_in, enc_upd_out, enc_gain,
    proc_msg_in, proc_msg_out, proc_upd_in, proc_upd_out, proc_gain,
):
    rows = g2m_weight.shape[1]
    width = grid_latent.shape[1]
    grid_blocks = grid_latent.shape[0] // rows
    blocks = mesh_latent.shape[0] // rows
    steps = proc_msg_in.shape[0]
    rim = halo_send.shape[1]
    peers = g2m_send.shape[1]
    hbm = pl.BlockSpec(memory_space=pl.ANY)

    sub = rows // PARTS
    flying = (grid_blocks, sub, width)
    staged = (3, 4, 4, 2, sub, width)
    holding = (4, 4, 4, 2, sub, width)
    dma = pltpu.SemaphoreType.DMA
    vm = pltpu.VMEM
    out = pl.pallas_call(
        whole_kernel,
        out_shape=jax.ShapeDtypeStruct((blocks, rows, width), BF16),
        in_specs=[hbm] * 20,
        out_specs=hbm,
        scratch_shapes=[
            *[vm(w.shape, BF16) for w in (
                enc_msg_in, enc_msg_out, enc_upd_in, enc_upd_out,
                proc_msg_in, proc_msg_out, proc_upd_in, proc_upd_out)],
            vm((1, width), F32),
            vm((steps, width), F32),
            vm((blocks, rows, width), BF16),
            *[vm(v.shape, jnp.int32) for v in (g2m_src, g2m_dst, m2m_src, m2m_dst, halo_send)],
            vm((8, 256), jnp.int32),
            pltpu.SMEM((8, 256), jnp.int32),
            vm((rows, rows, g2m_dst.shape[1]), BF16),
            vm((steps, rows, rows, m2m_dst.shape[1]), BF16),
            vm(g2m_weight.shape, BF16),
            vm((blocks, rows, rows * (g2m_dst.shape[1] // blocks)), BF16),
            vm((steps, blocks, rows, rows * (m2m_dst.shape[1] // blocks)), BF16),
            vm((5, 4, 2, 4, rows, width), BF16),
            *[vm(flying, BF16)] * 16,
            *[vm(staged, BF16)] * 4,
            *[vm(holding, BF16)] * 4,
            vm((blocks, rows, width), BF16),
            vm((blocks, rows, width), BF16),
            vm((2 * rim, rows, width), BF16),
            vm((2 * rim, rows, width), BF16),
            vm((rim, rows, width), BF16),
            vm((rim, rows, width), BF16),
            vm((1, peers), jnp.int32),
            vm((3, 4, 1, peers), jnp.int32),
            pltpu.SMEM((3, 4, 1, peers), jnp.int32),
            dma((8,)), dma((19,)), dma((3, 3)), dma((3, 3)),
            dma((4, 2, 2)), dma((4, 2, 2)), dma((4, 2)), dma((4, 2)),
            dma((4, 3, 4)), dma((4, 3, 4)), dma((4, 4, 8)), dma((4, 4, 8)), dma((4, 4)), dma((8,)),
            dma((steps, 2, 2)), dma((steps, 2, 2)),
        ],
        compiler_params=pltpu.CompilerParams(
            collective_id=0, has_side_effects=True, vmem_limit_bytes=62 * 2**20
        ),
        name="encoder_and_steps",
    )(
        g2m_src, g2m_dst, m2m_src, m2m_dst, halo_send,
        g2m_send, grid_latent.reshape(grid_blocks, rows, width), mesh_latent.reshape(blocks, rows, width),
        jnp.transpose(g2m_weight, (1, 2, 0)), jnp.transpose(m2m_weight, (0, 2, 3, 1)),
        enc_msg_in, enc_msg_out, enc_upd_in, enc_upd_out, enc_gain.reshape(1, width),
        proc_msg_in, proc_msg_out, proc_upd_in, proc_upd_out, proc_gain,
    )
    return out.reshape(blocks * rows, width)


def solution(mesh):
    both = P(("tile", "dom"), None)
    whole = P()
    placed = (
        both, both, both, both, both, P(("tile", "dom"), None, None), both, both, both,
        P(None, ("tile", "dom"), None, None),
    ) + (whole,) * 10
    return jax.shard_map(
        on_device, mesh=mesh, in_specs=placed, out_specs=both, check_vma=False
    )
```

```python
import functools

import jax
import jax.numpy as jnp
from jax import lax
from jax.experimental import pallas as pl
from jax.experimental.pallas import tpu as pltpu
from jax.sharding import PartitionSpec as P

MESH = pl.DeviceIdType.MESH
F32 = jnp.float32
BF16 = jnp.bfloat16


def silu(v):
    half = 0.5 * v
    return half + half * jnp.tanh(half)


def mm(a, b):
    return jnp.dot(a, b, preferred_element_type=F32)


def iota(shape, dim):
    return lax.broadcasted_iota(jnp.int32, shape, dim)


def total(mask, values, axis):
    return jnp.sum(jnp.where(mask, values, 0), axis=axis, keepdims=True)


def column(row):
    n = row.shape[1]
    return total(iota((n, n), 0) == iota((n, n), 1), row, 1)


def ranks(row):
    n = row.shape[1]
    key = row * n + iota((1, n), 1)
    return total(key < column(key), 1, 1)


def sort_by(rank, col):
    n = col.shape[0]
    return total(rank == iota((n, n), 1), col, 0)


def placed(place, row):
    n = place.shape[0]
    return total(iota((n, row.shape[1]), 0) == row, place, 0)


def loop(first, last, step):
    def body(i, _):
        step(i)
        return 0

    lax.fori_loop(first, last, body, 0)


PARTS = 4
LINES = (("x", "y", "z"), ("y", "z", "x"), ("z", "x", "y"), ("x", "y", "z"))
AXES = ("x", "y", "z")


def whole_kernel(
    g_src_h, g_dst_h, m_src_h, m_dst_h, halo_h,
    send_row, grid_latent, latent_in, g_weight, m_weight,
    a_in_h, a_out_h, e_in_h, e_out_h, e_gain_h, m_in_h, m_out_h, u_in_h, u_out_h, u_gain_h,
    out_h,
    a_in, a_out, e_in, e_out, m_in, m_out, u_in, u_out, e_gain, u_gain, latent,
    g_from, g_to, m_from, m_to, halo_of, index_v, index_s,
    lanes_g, lanes_m, raw, wt_g, wt_m, table,
    a00, a01, a02, a03, a10, a11, a12, a13, a20, a21, a22, a23, a30, a31, a32, a33,
    s0, s1, s2, s3, r0, r1, r2, r3,
    state, mine, ptable0, ptable1, payload0, payload1, own_row, rows_v, rows_s,
    chunk_sem, load_sem, row_s, row_r, ag_s, ag_r, relay_s, relay_r, mid_s, mid_r, last_s, last_r, keep_sem, local_sem,
    send_sem, recv_sem,
):
    blocks, rows, width = latent.shape
    grid_blocks = grid_latent.shape[0]
    sub = rows // PARTS
    rim = halo_of.shape[1]
    steps = m_in.shape[0]
    ptable, payload = (ptable0, ptable1), (payload0, payload1)
    ag = ((a00, a01, a02, a03), (a10, a11, a12, a13), (a20, a21, a22, a23), (a30, a31, a32, a33))
    stage, held = (s0, s1, s2, s3), (r0, r1, r2, r3)
    tile = lax.axis_index("tile")
    core = lax.rem(tile, 2)
    at = {"x": lax.axis_index("dom"), "y": lax.rem(tile // 2, 4), "z": tile // 8}

    def device(c, core_at):
        return (c["z"] * 4 + c["y"]) * 2 + core_at, c["x"]

    def moved(axis, by, flip=0):
        c = dict(at)
        c[axis] = lax.rem(at[axis] + by + 4, 4)
        return device(c, lax.rem(core + flip, 2))

    chunk = 4
    chunks = grid_blocks // chunk

    def chunk_load(h, i):
        n = h * (chunks // 2) + i
        return pltpu.make_async_copy(
            grid_latent.at[pl.ds(n * chunk, chunk)], (state, mine)[h].at[pl.ds(i * chunk, chunk)], chunk_sem.at[n])

    loads = [
        pltpu.make_async_copy(src, dst, load_sem.at[i])
        for i, (src, dst) in enumerate((
            (a_in_h, a_in), (a_out_h, a_out), (send_row, own_row),
            (g_src_h, g_from), (g_dst_h, g_to), (m_src_h, m_from), (m_dst_h, m_to), (halo_h, halo_of),
            (g_weight, lanes_g), (m_weight, lanes_m), (latent_in, latent), (e_gain_h, e_gain), (u_gain_h, u_gain),
            (e_in_h, e_in), (e_out_h, e_out), (m_in_h, m_in), (m_out_h, m_out), (u_in_h, u_in), (u_out_h, u_out),
        ))
    ]
    loads[0].start()
    chunk_load(0, 0).start()
    loads[1].start()
    loads[2].start()
    for i in range(1, chunks):
        chunk_load(i // (chunks // 2), i % (chunks // 2)).start()

    barrier = pltpu.get_barrier_semaphore()
    greeted = [moved(axis, by, flip) for axis in AXES for by in (1, 2, 3) for flip in (0, 1)] + [moved("x", 0, 1)]
    for peer in greeted:
        pl.semaphore_signal(barrier, inc=1, device_id=peer, device_id_type=MESH)

    def mlp(h, k):
        chunk_load(h, k).wait()
        i = h * (chunks // 2) + k
        x = (state, mine)[h][pl.ds(k * chunk, chunk)].reshape(chunk * rows, width)
        hidden = silu(mm(x, a_in[...])).astype(BF16)
        msg = mm(hidden, a_out[...]).astype(BF16).reshape(chunk, rows, width)
        table[0, i // 2, lax.rem(i, 2)] = msg
        for p in range(PARTS):
            ag[p][0][pl.ds(i * chunk, chunk)] = msg[:, p * sub:(p + 1) * sub]

    half = grid_blocks // 2

    def gather_copy(p, way, h):
        here = pl.ds(h * half, half)
        return pltpu.make_async_remote_copy(
            ag[p][0].at[here], ag[p][3 - 2 * way].at[here], ag_s.at[p, way, h], ag_r.at[p, way, h],
            device_id=moved(LINES[p][0], 1 - 2 * way), device_id_type=MESH)

    def relay_copy(p, way):
        here = pl.ds(way * half, half)
        return pltpu.make_async_remote_copy(
            ag[p][3 - 2 * way].at[here], ag[p][2].at[here], relay_s.at[p, way], relay_r.at[p, way],
            device_id=moved(LINES[p][0], 1 - 2 * way), device_id_type=MESH)

    def row_copy(a, by):
        axis = AXES[a]
        return pltpu.make_async_remote_copy(
            own_row, rows_v.at[a, at[axis]], row_s.at[a, by - 1], row_r.at[a, by - 1],
            device_id=moved(axis, by), device_id_type=MESH)

    loads[0].wait()
    loads[1].wait()
    loop(0, chunks // 2, functools.partial(mlp, 0))
    pl.semaphore_wait(barrier, len(greeted))
    for p in range(3):
        for way in (0, 1):
            gather_copy(p, way, 0).start()
    loads[2].wait()
    for a in range(3):
        for by in (1, 2, 3):
            row_copy(a, by).start()
    own_rows = [pltpu.make_async_copy(own_row, rows_v.at[a, at[AXES[a]]], local_sem.at[a]) for a in range(3)]
    for c in own_rows:
        c.start()
    loop(0, chunks // 2, functools.partial(mlp, 1))
    for p in range(3):
        for way in (0, 1):
            gather_copy(p, way, 1).start()

    for c in loads[3:]:
        c.start()

    def relays(p):
        for way in (0, 1):
            gather_copy(p, way, way).wait_recv()
            relay_copy(p, way).start()

    def near(p):
        for way in (0, 1):
            gather_copy(p, way, 1 - way).wait_recv()

    def far(p):
        for way in (0, 1):
            relay_copy(p, way).wait_recv()

    def spread(p):
        for h in (0, 1):
            for way in (0, 1):
                gather_copy(p, way, h).start()

    def spread_out(p):
        for way in (0, 1):
            relay_copy(p, way).wait_send()
            for h in (0, 1):
                gather_copy(p, way, h).wait_send()

    def held_at(p, b, j):
        return (j, b) if p == 2 else (b, j)

    def mid_copy(p, by, j):
        first, second, _ = LINES[p]
        b, k = held_at(p, at[second], lax.rem(at[first] + j, 4))
        return pltpu.make_async_remote_copy(
            stage[p].at[by - 1, j], held[p].at[b, k], mid_s.at[p, by - 1, j], mid_r.at[p, by - 1, j],
            device_id=moved(second, by), device_id_type=MESH)

    def select(p, js):
        first, second, third = LINES[p]
        a = AXES.index(first)

        def of(by, j):
            c = dict(at)
            c[second] = lax.rem(at[second] + by, 4)
            row = lax.rem(at[first] + j, 4)
            for k in range(8):
                c[third] = k // 2
                t, x = device(c, k % 2)
                yield k // 2, k % 2, ag[p][j][rows_s[a, row, 0, t * 4 + x]]

        for j in js:
            def put(by, _):
                for c3, k, got in of(by, j):
                    stage[p][by - 1, j, c3, k] = got
                return 0

            lax.fori_loop(1, 4, put, 0)
            b, row = held_at(p, at[second], lax.rem(at[first] + j, 4))
            for c3, k, got in of(0, j):
                held[p][b, row, c3, k] = got

    def pass_on(p, js):
        for j in js:
            for by in (1, 3, 2):
                mid_copy(p, by, j).start()

    def arrived(p, js):
        for j in js:
            loop(1, 4, lambda by: mid_copy(p, by, j).wait_recv())

    def landing(p, b):
        here = pl.ds(p * sub, sub)
        if p == 1:
            return table.at[1 + b, :, core, at["x"], here]
        if p == 2:
            return table.at[pl.ds(1, 4), at["y"], core, b, here]
        return table.at[1 + at["z"], b, core, :, here]

    def leaving(p, b, c3, k):
        return held[p].at[:, b, c3, k] if p == 2 else held[p].at[b, :, c3, k]

    def last_copy(p, bi, k):
        _, second, axis = LINES[p]
        by, flip = k // 2, lax.rem(k, 2)
        b = lax.rem(at[second] + bi, 4)
        return pltpu.make_async_remote_copy(
            leaving(p, b, lax.rem(at[axis] + by, 4), lax.rem(core + flip, 2)), landing(p, b),
            last_s.at[p, bi, k], last_r.at[p, bi, k],
            device_id=moved(axis, by, flip), device_id_type=MESH)

    def keep_copy(p, bi):
        _, second, axis = LINES[p]
        b = lax.rem(at[second] + bi, 4)
        return pltpu.make_async_copy(leaving(p, b, at[axis], core), landing(p, b), keep_sem.at[p, bi])

    def deliver(p, first, last):
        def one(bi):
            loop(1, 8, lambda k: last_copy(p, bi, k).start())
            keep_copy(p, bi).start()

        loop(first, last, one)

    slots_g = g_to.shape[1] // blocks
    slots_m = m_to.shape[1] // blocks
    packed = 16

    def listed(r):
        return lambda k: index_s[r, k]

    g_order, g_src, m_order, m_src, perm, place, halo_at = [listed(r) for r in range(7)]

    def index_lists():
        halo_row = halo_of[...]
        named = iota((blocks, rim), 0) == halo_row
        first = jnp.min(
            jnp.where(named, iota((blocks, rim), 1), rim + iota((blocks, rim), 0)), axis=1, keepdims=True)
        first_row = total(iota((blocks, blocks), 0) == iota((blocks, blocks), 1), first, 0)
        spot = total(first_row < first, 1, 1)
        rank_g = ranks(placed(spot, g_to[...]))
        rank_m = ranks(placed(spot, m_to[...]))
        m_row = m_from[...]
        own = jnp.where(m_row < blocks, placed(spot, jnp.minimum(m_row, blocks - 1)), m_row)
        ng, nm = g_to.shape[1], m_to.shape[1]
        for r, row in enumerate((
            sort_by(rank_g, iota((ng, 1), 0)), sort_by(rank_g, column(g_from[...])),
            sort_by(rank_m, iota((nm, 1), 0)), sort_by(rank_m, column(own)),
            sort_by(spot, iota((blocks, 1), 0)),
            total(iota((blocks, blocks), 0) == iota((blocks, blocks), 1), spot, 0),
            placed(spot, halo_row),
        )):
            index_v[pl.ds(r, 1), pl.ds(0, row.shape[1])] = row
        copy = pltpu.make_async_copy(index_v, index_s, local_sem.at[7])
        copy.start()
        return copy

    def unpack(lanes, base, first, last):
        def body(q, _):
            x = lanes[pl.ds(q * packed, packed)]
            tiles = jnp.swapaxes(jnp.swapaxes(x, 1, 2), 0, 1)
            raw[pl.ds(base, tiles.shape[0]), pl.ds(q * packed, packed)] = tiles
            return 0
        lax.fori_loop(first, last, body, 0)

    def prepare(order, base, wt, slots):
        def body(b, _):
            cat = jnp.concatenate([raw[base + order(b * slots + k)] for k in range(slots)], axis=0)
            wt[b] = cat.T
            return 0
        lax.fori_loop(0, blocks, body, 0)

    def rim_weights(s, base, h):
        side = iota((rows, 2 * rows), 1) // rows
        wide = 2 * rows

        def one(n):
            b = h * (blocks // 2) + n
            src = [m_src(b * slots_m + k) for k in range(slots_m)]
            tiles = [raw[base + m_order(b * slots_m + k)] for k in range(slots_m)]
            own = [jnp.where(src[k] < blocks, tiles[k], jnp.zeros_like(tiles[k])) for k in range(slots_m)]
            wt_m[s, b] = jnp.concatenate(own, axis=0).T
            twice = jnp.concatenate([t for t in tiles for _ in (0, 1)], axis=0).T.astype(F32)
            for pair in range(rim):
                acc = jnp.zeros((rows, wide), F32)
                for k in range(slots_m):
                    hit = side + (blocks + 2 * pair) == src[k]
                    acc = acc + jnp.where(hit, twice[:, k * wide:(k + 1) * wide], 0.0)
                q, lane = pair // (rim // 2), pair % (rim // 2)
                ag[s][2 * q + h][pl.ds(n * PARTS, PARTS), :, pl.ds(lane * wide, wide)] = (
                    acc.astype(BF16).reshape(PARTS, sub, wide))

        loop(0, blocks // 2, one)

    groups = rows // packed
    for c in loads[3:8]:
        c.wait()
    lists = index_lists()
    loads[8].wait()
    unpack(lanes_g, 0, 0, 2)
    for p in range(3):
        relays(p)
    unpack(lanes_g, 0, 2, groups)
    for a in range(3):
        own_rows[a].wait()
        for by in (1, 2, 3):
            row_copy(a, by).wait()
    to_scalar = pltpu.make_async_copy(rows_v, rows_s, local_sem.at[0])
    to_scalar.start()
    to_scalar.wait()
    lists.wait()

    every, close = (0, 1, 3, 2), (0, 1, 3)
    select(0, (0,))
    select(1, (0,))
    near(0)
    spread(3)
    select(0, (1, 3))
    pass_on(0, close)
    near(1)
    select(1, (1, 3))
    pass_on(1, close)
    near(2)
    select(2, close)
    far(0)
    select(0, (2,))
    pass_on(0, (2,))
    far(1)
    select(1, (2,))
    pass_on(1, (2,))
    prepare(g_order, 0, wt_g, slots_g)
    far(2)
    select(2, (2,))
    relays(3)
    loads[9].wait()
    half_tiles = raw.shape[0] // steps
    unpack(lanes_m.at[0], 0, 0, groups)
    select(3, (0,))
    near(3)
    pass_on(2, every)
    select(3, (1, 3))
    deliver(0, 0, 1)
    unpack(lanes_m.at[1], half_tiles, 0, groups)
    far(3)
    select(3, (2,))
    pass_on(3, every)
    for p in range(2):
        spread_out(p)
    rim_weights(0, 0, 0)
    arrived(0, every)
    deliver(0, 1, 4)
    rim_weights(0, 0, 1)
    rim_weights(1, half_tiles, 0)
    arrived(1, every)
    arrived(2, close)
    deliver(1, 0, 4)
    deliver(3, 0, 1)
    rim_weights(1, half_tiles, 1)
    arrived(2, (2,))
    deliver(2, 0, 4)
    arrived(3, every)
    deliver(3, 1, 4)
    for c in loads[10:]:
        c.wait()
    for p in range(PARTS):
        def landed(bi):
            loop(1, 8, lambda k: last_copy(p, bi, k).wait_recv())
            keep_copy(p, bi).wait()

        loop(0, 4, landed)

    n_dom = lax.axis_size("dom")
    upper, lower = moved("x", 1), moved("x", 3)
    quarter = blocks // 4
    pieces = ((0, 2), (2, 2), (4, rim - 4))

    def halo(s, h):
        src = payload[s].at[pl.ds(*pieces[h])]
        up = pltpu.make_async_remote_copy(
            src, ptable[s].at[pl.ds(*pieces[h])],
            send_sem.at[s, 0, h], recv_sem.at[s, 0, h], device_id=upper, device_id_type=MESH)
        down = pltpu.make_async_remote_copy(
            src, ptable[s].at[pl.ds(rim + pieces[h][0], pieces[h][1])],
            send_sem.at[s, 1, h], recv_sem.at[s, 1, h], device_id=lower, device_id_type=MESH)
        return up, down

    def from_grid(i):
        return table[i // 32, lax.rem(i // 8, 4), lax.rem(i // 4, 2), lax.rem(i, 4)]

    def tiles_sum(load, idx, wt, slots, p):
        got = jnp.concatenate([load(idx(p * slots + k)) for k in range(slots)], axis=0)
        return mm(wt[p], got)

    def own_part(s):
        def one(p):
            acc = tiles_sum(lambda i: mine[jnp.minimum(i, blocks - 1)], m_src, wt_m.at[s], slots_m, p)
            high = acc.astype(BF16)
            at_p = p // 8, lax.rem(p // 4, 2), lax.rem(p, 4)
            table[(0, *at_p)] = high
            table[(1, *at_p)] = (acc - high.astype(F32)).astype(BF16)

        loop(0, blocks, one)

    def rim_part(s, h, k, n):
        some = pl.ds(k * PARTS, n * PARTS)
        acc = jnp.zeros((n * rows, width), F32)
        for q in (0, 1):
            dense = ag[s][2 * q + h][some].reshape(n * rows, rim * rows)
            acc = acc + mm(dense, ptable[s][pl.ds(q * rim, rim)].reshape(rim * rows, width))
        for level in (0, 1):
            acc = acc + table[level, h, k // 4, pl.ds(lax.rem(k, 4), n)].reshape(n * rows, width).astype(F32)
        return acc.astype(BF16)

    def update(old, agg, w_in, w_out, gain):
        pre = mm(old, w_in[pl.ds(0, width), :]) + mm(agg, w_in[pl.ds(width, width), :])
        o = mm(silu(pre).astype(BF16), w_out[...])
        mean = jnp.mean(o, axis=1, keepdims=True)
        cen = o - mean
        var = jnp.mean(cen * cen, axis=1, keepdims=True)
        normed = cen * lax.rsqrt(var + 1e-05) * gain
        return (old.astype(F32) + normed).astype(BF16)

    def message(s, first, n, new):
        h = silu(mm(new, m_in[s])).astype(BF16)
        msg = mm(h, m_out[s]).astype(BF16)
        mine[pl.ds(first, n)] = msg.reshape(n, rows, width)

    def push(s, h):
        first, count = pieces[h]
        for i in range(first, first + count):
            payload[s][i] = mine[halo_at(i)]
        for c in halo(s, h):
            c.start()

    def enc_chunk(first, n):
        agg = jnp.concatenate([
            tiles_sum(from_grid, g_src, wt_g, slots_g, first + i).astype(BF16) for i in range(n)], axis=0)
        old = jnp.concatenate([latent[perm(first + i)] for i in range(n)], axis=0)
        new = update(old, agg, e_in, e_out, e_gain[...])
        state[pl.ds(first, n)] = new.reshape(n, rows, width)
        message(0, first, n, new)

    def proc_chunk(s, h, k, n):
        first = h * (blocks // 2) + k
        old = state[pl.ds(first, n)].reshape(n * rows, width)
        new = update(old, rim_part(s, h, k, n), u_in.at[s], u_out.at[s], u_gain[pl.ds(s, 1), :])
        state[pl.ds(first, n)] = new.reshape(n, rows, width)
        if s + 1 < steps:
            message(s + 1, first, n, new)

    for h, (first, n) in enumerate(pieces):
        enc_chunk(first, n)
        push(0, h)
    loop(2, 4, lambda c: enc_chunk(c * quarter, quarter))
    for s in range(steps):
        own_part(s)
        for h in range(len(pieces)):
            for c in halo(s, h):
                c.wait()
        if s + 1 < steps:
            for h, (first, n) in enumerate(pieces):
                proc_chunk(s, 0, first, n)
                push(s + 1, h)
            loop(0, 2, lambda c: proc_chunk(s, 1, c * quarter, quarter))
        else:
            for h in (0, 1):
                proc_chunk(s, h, 0, quarter)
                proc_chunk(s, h, quarter, quarter)

    def restore(b, _):
        mine[b] = state[place(b)]
        return 0

    lax.fori_loop(0, blocks, restore, 0)
    store = pltpu.make_async_copy(mine, out_h, local_sem.at[0])
    store.start()
    for p in range(PARTS):
        if p >= 2:
            spread_out(p)

        def sent(j):
            loop(1, 4, lambda by: mid_copy(p, by, j).wait_send())
            loop(1, 8, lambda k: last_copy(p, j, k).wait_send())

        loop(0, 4, sent)
    store.wait()


def on_device(
    grid_latent, mesh_latent, g2m_send, g2m_src, g2m_dst, g2m_weight, halo_send, m2m_src, m2m_dst, m2m_weight,
    enc_msg_in, enc_msg_out, enc_upd_in, enc_upd_out, enc_gain,
    proc_msg_in, proc_msg_out, proc_upd_in, proc_upd_out, proc_gain,
):
    rows = g2m_weight.shape[1]
    width = grid_latent.shape[1]
    grid_blocks = grid_latent.shape[0] // rows
    blocks = mesh_latent.shape[0] // rows
    steps = proc_msg_in.shape[0]
    rim = halo_send.shape[1]
    peers = g2m_send.shape[1]
    hbm = pl.BlockSpec(memory_space=pl.ANY)

    sub = rows // PARTS
    flying = (grid_blocks, sub, width)
    staged = (3, 4, 4, 2, sub, width)
    holding = (4, 4, 4, 2, sub, width)
    dma = pltpu.SemaphoreType.DMA
    vm = pltpu.VMEM
    out = pl.pallas_call(
        whole_kernel,
        out_shape=jax.ShapeDtypeStruct((blocks, rows, width), BF16),
        in_specs=[hbm] * 20,
        out_specs=hbm,
        scratch_shapes=[
            *[vm(w.shape, BF16) for w in (
                enc_msg_in, enc_msg_out, enc_upd_in, enc_upd_out,
                proc_msg_in, proc_msg_out, proc_upd_in, proc_upd_out)],
            vm((1, width), F32),
            vm((steps, width), F32),
            vm((blocks, rows, width), BF16),
            *[vm(v.shape, jnp.int32) for v in (g2m_src, g2m_dst, m2m_src, m2m_dst, halo_send)],
            vm((8, 256), jnp.int32),
            pltpu.SMEM((8, 256), jnp.int32),
            vm((rows, rows, g2m_dst.shape[1]), BF16),
            vm((steps, rows, rows, m2m_dst.shape[1]), BF16),
            vm(g2m_weight.shape, BF16),
            vm((blocks, rows, rows * (g2m_dst.shape[1] // blocks)), BF16),
            vm((steps, blocks, rows, rows * (m2m_dst.shape[1] // blocks)), BF16),
            vm((5, 4, 2, 4, rows, width), BF16),
            *[vm(flying, BF16)] * 16,
            *[vm(staged, BF16)] * 4,
            *[vm(holding, BF16)] * 4,
            vm((blocks, rows, width), BF16),
            vm((blocks, rows, width), BF16),
            vm((2 * rim, rows, width), BF16),
            vm((2 * rim, rows, width), BF16),
            vm((rim, rows, width), BF16),
            vm((rim, rows, width), BF16),
            vm((1, peers), jnp.int32),
            vm((3, 4, 1, peers), jnp.int32),
            pltpu.SMEM((3, 4, 1, peers), jnp.int32),
            dma((8,)), dma((19,)), dma((3, 3)), dma((3, 3)),
            dma((4, 2, 2)), dma((4, 2, 2)), dma((4, 2)), dma((4, 2)),
            dma((4, 3, 4)), dma((4, 3, 4)), dma((4, 4, 8)), dma((4, 4, 8)), dma((4, 4)), dma((8,)),
            dma((steps, 2, 3)), dma((steps, 2, 3)),
        ],
        compiler_params=pltpu.CompilerParams(
            collective_id=0, has_side_effects=True, vmem_limit_bytes=62 * 2**20
        ),
        name="encoder_and_steps",
    )(
        g2m_src, g2m_dst, m2m_src, m2m_dst, halo_send,
        g2m_send, grid_latent.reshape(grid_blocks, rows, width), mesh_latent.reshape(blocks, rows, width),
        jnp.transpose(g2m_weight, (1, 2, 0)), jnp.transpose(m2m_weight, (0, 2, 3, 1)),
        enc_msg_in, enc_msg_out, enc_upd_in, enc_upd_out, enc_gain.reshape(1, width),
        proc_msg_in, proc_msg_out, proc_upd_in, proc_upd_out, proc_gain,
    )
    return out.reshape(blocks * rows, width)


def solution(mesh):
    both = P(("tile", "dom"), None)
    whole = P()
    placed = (
        both, both, both, both, both, P(("tile", "dom"), None, None), both, both, both,
        P(None, ("tile", "dom"), None, None),
    ) + (whole,) * 10
    return jax.shard_map(
        on_device, mesh=mesh, in_specs=placed, out_specs=both, check_vma=False
    )
```
